512 devices in a mesh: beam: 32 (over x, y, core), freq: 16 (over z).
Axes of the slice: x: 4, y: 4, z: 16, core: 2. Of those that a mesh axis runs over, the one named last changes fastest.
Arguments:
- voltages: bfloat16 [2048, 1024, 256], P(('beam', 'freq')), may hold values from -6 to 6
- gains: float32 [2048, 2, 1024], P(('beam', 'freq')), may hold values from -6 to 6
- channel_map: int32 [2048], P(('beam', 'freq')), may hold values from 0 to 2047, as said below
- positions: float32 [2, 1024], replicated, may hold values from -4 to 4
- directions: float32 [2, 256], replicated, may hold values from -0.5 to 0.5
- local_delay: int32 [256, 128], P('freq'), may hold values from 0 to 16
- merge_table: int32 [3, 480], replicated, may hold values from 0 to 127, as said below
Outputs:
- dedispersed: float32 [256, 256, 128], P('freq', 'beam')
The draws below stay inside these ranges and needn't reach their ends.
Inputs may be any that keep to these rules, and one draw needn't show every extreme that they name: `channel_map`: stored channels (i * 16 + f) * 4 + l over all i and l hold the sky channels f * 128 to (f + 1) * 128 - 1, each once. `merge_table`: in merge step k (entries 2 * 16 * (2^k - 1) to 2 * 16 * (2^(k+1) - 1) - 1), the two row numbers are below 16 * 2^k and every row number appears; delays run from 0 to 24, each value appearing.
All inputs are finite; a program needn't handle non-finite values.
Results may differ from the reference program's by a relative error of at most 0.005.
Values may be sent and summed in bfloat16 or wider, within the bound.
A program may use at most 128 MiB of HBM per device.

```python
import math
import jax
import jax.numpy as jnp
from jax import lax

ANTENNA_COUNT = 1024
BEAMS = 256
TIME_SAMPLES = 128
DEVICE_CHANNELS = 4
R0 = 16
LOCAL_MAX = 16
SHIFT_MAX = 24
CHANNEL_COUNT = 2048
CH_SUB = 128
DMS = 256
N_BEAM = 32
N_FREQ = 16


def draw_channel_map(key, part):
    key = jax.random.fold_in(key, 11)
    subbands = CHANNEL_COUNT // CH_SUB
    senders = CH_SUB // DEVICE_CHANNELS

    def order_of(number):
        return jax.random.permutation(jax.random.fold_in(key, number), CH_SUB)
    orders = jax.vmap(order_of)(jnp.arange(subbands))
    sky = orders + (jnp.arange(subbands) * CH_SUB)[:, None]
    return sky.reshape(subbands, senders, DEVICE_CHANNELS).transpose(1, 0, 2).reshape(CHANNEL_COUNT).astype(jnp.int32)


def draw_merge_table(key, part):
    key = jax.random.fold_in(key, 23)
    section_count = (DMS // R0).bit_length() - 1
    pieces = []
    for section in range(section_count):
        row_count = R0 * 2 ** section
        new_rows = 2 * row_count
        lower_rows = jax.random.permutation(jax.random.fold_in(key, 3 * section), new_rows) % row_count
        upper_rows = jax.random.permutation(jax.random.fold_in(key, 3 * section + 1), new_rows) % row_count
        shifts = jax.random.permutation(jax.random.fold_in(key, 3 * section + 2), new_rows) % (SHIFT_MAX + 1)
        pieces.append(jnp.stack([lower_rows, upper_rows, shifts]))
    return jnp.concatenate(pieces, axis=1).astype(jnp.int32)


def place_ends(values, rng, smallest, top_value):
    spot = [jax.random.randint(jax.random.fold_in(rng, axis), (), 0, length) for axis, length in enumerate(values.shape)]
    longest = values.shape.index(max(values.shape))
    neighbour = spot[:longest] + [(spot[longest] + 1) % values.shape[longest]] + spot[longest + 1:]
    return values.at[tuple(spot)].set(smallest).at[tuple(neighbour)].set(top_value)


def levels(rng, dims, cuts, smallest, top_value):
    loudness, own = 1.0, jax.random.fold_in(rng, 6)
    for dim, blocks in cuts:
        steps = jnp.exp(jax.random.uniform(jax.random.fold_in(own, dim), (blocks,), jnp.float32, smallest / len(cuts), top_value / len(cuts)))
        loudness = loudness * jnp.repeat(steps, dims[dim] // blocks).reshape([-1 if axis == dim else 1 for axis in range(len(dims))])
    return loudness


def noise(key, shape, width, limit, cuts=(), kind=jnp.bfloat16):
    entries = jax.random.normal(key, shape, jnp.float32) * width
    if len(cuts) > 0:
        entries = levels(key, shape, cuts, -0.22, 0.18) * entries
    return jnp.clip(entries, min=-limit, max=limit).astype(kind)


def setup_inputs(seed: int = 0) -> dict:
    key_of = jax.random.split(jax.random.key(seed), 8)
    return {
        "voltages": noise(key_of[0], (CHANNEL_COUNT, ANTENNA_COUNT, 2 * TIME_SAMPLES), 1.0, 6.0, ((0, 512),)),
        "gains": noise(key_of[1], (CHANNEL_COUNT, 2, ANTENNA_COUNT), 1.0, 6.0, ((0, 512),), jnp.float32),
        "channel_map": draw_channel_map(jax.random.fold_in(key_of[7], 71), 0),
        "positions": jnp.clip(jax.random.uniform(key_of[3], (2, ANTENNA_COUNT), jnp.float32, -4.0, 4.0), -4.0, 4.0),
        "directions": jnp.clip(jax.random.uniform(key_of[4], (2, BEAMS), jnp.float32, -0.5, 0.5), -0.5, 0.5),
        "local_delay": place_ends(jax.random.randint(key_of[5], (DMS, CH_SUB), 0, LOCAL_MAX + 1), jax.random.fold_in(key_of[5], 1), 0, LOCAL_MAX).astype(jnp.int32),
        "merge_table": draw_merge_table(jax.random.fold_in(key_of[7], 71), 0),
    }


def beam_power(volts, gain_pair, sky_channel, geometry, total_channels):
    ratio = 1.0 + sky_channel / total_channels
    angle = 2.0 * math.pi * ratio * geometry
    factor = 1.0 / math.sqrt(geometry.shape[1])
    amplitude = jnp.sqrt(gain_pair[0] * gain_pair[0] + gain_pair[1] * gain_pair[1]) * factor
    phase = jnp.arctan2(gain_pair[1], gain_pair[0])
    base = angle - phase[None, :]
    turned = jnp.concatenate([base, base + 0.5 * math.pi], axis=0)
    stacked = (amplitude[None, :] * jnp.cos(turned)).astype(jnp.bfloat16)
    product = jnp.dot(stacked.astype(jnp.float32), volts.astype(jnp.float32), preferred_element_type=jnp.float32)
    beam_count = geometry.shape[0]
    samples = volts.shape[1] // 2
    beam_re = product[:beam_count, :samples] - product[beam_count:, samples:]
    beam_im = product[:beam_count, samples:] + product[beam_count:, :samples]
    power = beam_re * beam_re + beam_im * beam_im
    return (0.25 * (power - lax.optimization_barrier(jnp.mean(power, axis=1, keepdims=True)))).astype(jnp.bfloat16)

def local_sum(columns, delays):
    samples = columns.shape[2]
    padded = jnp.pad(columns, ((0, 0), (0, 0), (LOCAL_MAX, 0)))

    def slide_row(plane_row, offset):
        return lax.dynamic_slice_in_dim(plane_row, LOCAL_MAX - offset, samples, 1)

    def one_trial(row_delays):
        moved = jax.vmap(slide_row)(padded, row_delays)
        return lax.optimization_barrier(jnp.sum(moved.astype(jnp.float32), axis=0))
    return lax.map(one_trial, delays)

def merge_pair(lower, higher, lower_rows, upper_rows, shifts):
    samples = lower.shape[2]
    from_lower = jnp.take(lower, lower_rows, axis=0)
    from_upper = jnp.take(higher, upper_rows, axis=0)
    padded = jnp.pad(from_upper, ((0, 0), (0, 0), (SHIFT_MAX, 0)))

    def slide_row(plane_row, offset):
        return lax.dynamic_slice_in_dim(plane_row, SHIFT_MAX - offset, samples, 1)
    return from_lower + jax.vmap(slide_row)(padded, shifts)

def reference(voltages, gains, channel_map, positions, directions, local_delay, merge_table):
    geometry = directions[0][:, None] * positions[0][None, :] + directions[1][:, None] * positions[1][None, :]

    def channel_share(packed):
        return beam_power(packed[0], packed[1], packed[2], geometry, CHANNEL_COUNT)
    intensity = lax.map(channel_share, (voltages, gains, channel_map.astype(jnp.float32)))
    grouped = intensity.reshape(N_BEAM, N_FREQ, DEVICE_CHANNELS, BEAMS, TIME_SAMPLES).transpose(1, 0, 2, 3, 4).reshape(N_FREQ, CH_SUB, BEAMS, TIME_SAMPLES)
    delays = local_delay.reshape(N_FREQ, R0, CH_SUB)

    def per_subband(packed):
        return local_sum(packed[0], packed[1])
    partial_value = lax.map(per_subband, (grouped, delays)).reshape(N_FREQ * R0, BEAMS, TIME_SAMPLES)
    section_count = N_FREQ.bit_length() - 1
    state = partial_value
    for section in range(section_count):
        group_count = N_FREQ >> section
        row_count = R0 << section
        start = 2 * R0 * (2 ** section - 1)
        table = merge_table[:, start:start + 2 * row_count]
        paired = state.reshape(group_count // 2, 2, row_count, BEAMS, TIME_SAMPLES)

        def group_share(pair_state):
            return merge_pair(pair_state[0], pair_state[1], table[0], table[1], table[2])
        state = jax.vmap(group_share)(paired).reshape(group_count // 2 * 2 * row_count, BEAMS, TIME_SAMPLES)
    return state * (1.0 / math.sqrt(CHANNEL_COUNT))
```

```python
import functools
import math

import jax
import jax.numpy as jnp
from jax import lax
from jax.experimental import pallas as pl
from jax.experimental.pallas import tpu as pltpu
from jax.sharding import PartitionSpec as P

MESH = pl.DeviceIdType.MESH
F32 = jnp.float32
BF16 = jnp.bfloat16

CHANNELS = 4
ANTENNAS = 1024
BEAMS = 256
SAMPLES = 128
SENDERS = 32
GROUP = 8
GROUPS = SENDERS // GROUP
TURNS = 2
TURN_BEAMS = BEAMS // TURNS
TURN_SENDS = SENDERS // TURNS
OWN_BEAMS = BEAMS // SENDERS
TRIALS = 16
OFFSETS = 17
SUBBANDS = 16
REACH = 2
PLACES = 2 * REACH + 2
NEARS = PLACES - 1
FARS = 2
ENTRIES = 480

SIN_TERMS = (2.22143036, -0.91317465, 0.10983828)
ROUNDER = 12582912.0


def horner(terms, z):
    total = z * terms[-1] + terms[-2]
    for term in terms[-3::-1]:
        total = total * z + term
    return total


def weight_pair(geometry, ratio, gain_re, gain_im):
    turns = geometry * ratio
    rest = turns - ((turns + ROUNDER) - ROUNDER)
    z = rest * rest
    quarter_sin = rest * horner(SIN_TERMS, z)
    square = quarter_sin * quarter_sin
    left = 2.0 - square
    half_sin = quarter_sin * (left * lax.rsqrt(left))
    half_cos = 1.0 - square
    doubled = half_sin + half_sin
    cosine = 1.0 - doubled * half_sin
    sine = doubled * half_cos
    return gain_re * cosine + gain_im * sine, gain_im * cosine - gain_re * sine


def kernel(
    volts_hbm, gains_hbm, channel_hbm, positions_hbm, directions_hbm, delay_hbm, merge_hbm, out_ref,
    gains_ref, channel_ref, positions_ref, directions_ref, delay_ref, merge_ref, volts, geometry, across, intensity, outgoing, incoming, rows_f32, columns,
    selector, partial_f32, window, own_block, window_in, sums_out, sums_in, table_pad, table_vmem, table,
    small_sem, volts_sem, table_sem, send_sem, recv_sem, near_send, near_recv, far_send, far_recv,
):
    beam_at = lax.axis_index("beam")
    freq_at = lax.axis_index("freq")
    row = beam_at // GROUP
    spot = lax.rem(beam_at // 2, GROUPS)
    core = lax.rem(beam_at, 2)
    lean = 1 - 2 * core

    def ring(offset):
        return lax.rem(freq_at + offset + SUBBANDS, SUBBANDS)

    def mate(distance, step, to_core):
        return lax.rem(row + distance, GROUPS) * GROUP + lax.rem(spot + step, GROUPS) * 2 + to_core

    smalls = [
        pltpu.make_async_copy(src, dst, small_sem.at[n])
        for n, (src, dst) in enumerate((
            (merge_hbm, merge_ref), (directions_hbm, directions_ref), (positions_hbm, positions_ref),
            (gains_hbm, gains_ref), (channel_hbm, channel_ref), (delay_hbm, delay_ref),
        ))
    ]
    for small in smalls:
        small.start()
    loads = [
        pltpu.make_async_copy(volts_hbm.at[c], volts.at[c], volts_sem.at[c]) for c in range(CHANNELS)
    ]
    for load in loads:
        load.start()

    barrier = pltpu.get_barrier_semaphore()

    for step in range(1, SENDERS):
        other = lax.rem(beam_at + step, SENDERS)
        pl.semaphore_signal(barrier, inc=1, device_id=(other, freq_at), device_id_type=MESH)
    near_offsets = (-2, 2, -1, 1, 3 * lean)
    far_offsets = (6 * lean, -5 * lean)
    for offset in near_offsets + far_offsets:
        pl.semaphore_signal(barrier, inc=1, device_id=(beam_at, ring(offset)), device_id_type=MESH)

    for small in smalls:
        small.wait()

    for k in range(2):
        across[k] = jnp.transpose(jnp.broadcast_to(directions_ref[k : k + 1, :], (128, BEAMS)))

    def geometry_rows(chip, carry):
        for to_core in range(2):
            at = pl.ds(pl.multiple_of(chip * 16 + to_core * 8, 8), 8)
            to = pl.ds(pl.multiple_of(to_core * (BEAMS // 2) + chip * 8, 8), 8)
            first, second = across[0, at, :], across[1, at, :]
            for n in range(ANTENNAS // 128):
                lanes = pl.ds(n * 128, 128)
                geometry[to, lanes] = (
                    first * positions_ref[0:1, lanes] + second * positions_ref[1:2, lanes]
                )
        return carry

    lax.fori_loop(0, SENDERS // 2, geometry_rows, 0)
    for load in loads:
        load.wait()

    half_width = ANTENNAS // 2

    def beams_of(to_core):
        for c in range(CHANNELS):
            ratio = 1.0 + channel_ref[c].astype(F32) * (1.0 / 2048.0)
            product = None
            for half in range(2):
                lanes = pl.ds(half * half_width, half_width)
                gain_re = jnp.broadcast_to(gains_ref[c, 0:1, lanes] * (1.0 / 32.0), (16, half_width))
                gain_im = jnp.broadcast_to(gains_ref[c, 1:2, lanes] * (1.0 / 32.0), (16, half_width))
                real, imag = [], []
                for n in range(TURN_BEAMS // 16):
                    at = pl.ds(pl.multiple_of(to_core * (BEAMS // 2) + n * 16, 16), 16)
                    pair = weight_pair(geometry[at, lanes], ratio, gain_re, gain_im)
                    real.append(pair[0].astype(BF16))
                    imag.append(pair[1].astype(BF16))
                weights = jnp.concatenate(real + imag, axis=0)
                term = jnp.dot(weights, volts[c, lanes, :], preferred_element_type=F32)
                product = term if product is None else product + term
            beam_re = product[:TURN_BEAMS, :SAMPLES] - product[TURN_BEAMS:, SAMPLES:]
            beam_im = product[:TURN_BEAMS, SAMPLES:] + product[TURN_BEAMS:, :SAMPLES]
            power = beam_re * beam_re + beam_im * beam_im
            mean = jnp.sum(power, axis=1, keepdims=True) * (1.0 / SAMPLES)
            intensity[c] = 0.25 * (power - mean)
        for n in range(TURN_SENDS):
            for pair in range(CHANNELS // 2):
                rows = jnp.concatenate(
                    [intensity[2 * pair + c, n * OWN_BEAMS : (n + 1) * OWN_BEAMS, :] for c in range(2)], axis=0
                )
                outgoing[2 * n + to_core, pair * 16 : (pair + 1) * 16, :] = rows.astype(BF16)

    def shipment(distance, step, to_core):
        to = mate(distance, step, to_core)
        slot = (distance * GROUPS + step) * 2 + core
        return pltpu.make_async_remote_copy(
            src_ref=outgoing.at[to],
            dst_ref=incoming.at[slot],
            send_sem=send_sem,
            recv_sem=recv_sem.at[distance // 2],
            device_id=(to, freq_at),
            device_id_type=MESH,
        )

    def beams_and_send(to_core, carry):
        beams_of(to_core)

        @pl.when(to_core == 0)
        def _():
            pl.semaphore_wait(barrier, SENDERS - 1 + NEARS + FARS)

        for distance in range(GROUPS - 1, -1, -1):
            for step in range(GROUPS):
                if distance > 0 or step > 0:
                    shipment(distance, step, to_core).start()

        @pl.when(to_core != core)
        def _():
            shipment(0, 0, to_core).start()

        return carry

    lax.fori_loop(0, TURNS, beams_and_send, 0)
    keep = pltpu.make_async_copy(outgoing.at[beam_at], incoming.at[core], recv_sem.at[0])
    keep.start()

    lane = lax.broadcasted_iota(jnp.int32, (8, 128), 1)
    table_pad[...] = jnp.zeros_like(table_pad)
    table_pad[0:3, 0:ENTRIES] = merge_ref[...]
    code = table_pad[0:1, :] + 128 * table_pad[1:2, :] + 16384 * table_pad[2:3, :]
    pieces = [jnp.broadcast_to(code[:, 128 * n : 128 * (n + 1)], (8, 128)) for n in range(4)]
    turned = [pltpu.roll(piece, 32, 1) for piece in pieces]
    level_zero = pieces[0]
    level_one = pltpu.roll(pieces[0], 96, 1)
    level_two = jnp.where(lane < 32, turned[0], turned[1])
    last = [jnp.where(lane < 32, turned[1], turned[2]), jnp.where(lane < 32, turned[2], turned[3])]
    for part in range(2):
        subband = part * 8 + lax.broadcasted_iota(jnp.int32, (8, 128), 0)
        for half in range(2):
            found = last[half]
            late = jnp.zeros((8, 128), jnp.int32)
            for bit, level in ((3, level_two), (2, level_one), (1, level_zero), (0, None)):
                upper = lax.rem(jnp.right_shift(subband, bit), 2) == 1
                at = jnp.where(upper, jnp.right_shift(found, 7), found) & 127
                late = late + jnp.where(upper, jnp.right_shift(found, 14), 0)
                if level is not None:
                    found = jnp.take_along_axis(level, at, axis=1, mode="promise_in_bounds")
            table_vmem[pl.ds(part * 8, 8), pl.ds(half * 128, 128)] = at * 128 + late
    to_scalars = pltpu.make_async_copy(table_vmem, table, table_sem)
    to_scalars.start()

    channel = (
        ((row + GROUPS - jnp.right_shift(lane, 5)) & (GROUPS - 1)) * (GROUP * CHANNELS)
        + ((spot + GROUPS - (jnp.right_shift(lane, 3) & (GROUPS - 1))) & (GROUPS - 1)) * (2 * CHANNELS)
        + (jnp.right_shift(lane, 2) & 1) * CHANNELS
        + (lane & (CHANNELS - 1))
    )
    delays = jnp.concatenate(
        [
            jnp.take_along_axis(delay_ref[8 * n : 8 * n + 8, :], channel, axis=1, mode="promise_in_bounds")
            for n in range(TRIALS // 8)
        ],
        axis=0,
    )
    selector[...] = jnp.concatenate(
        [jnp.where(delays == n, 1.0, 0.0) for n in range(OFFSETS)], axis=0
    ).astype(BF16)

    half_way = SENDERS // 2

    def all_blocks(first, count):
        return pltpu.make_async_remote_copy(
            src_ref=outgoing.at[pl.ds(first, count)],
            dst_ref=incoming.at[pl.ds(first, count)],
            send_sem=send_sem,
            recv_sem=recv_sem.at[first // half_way],
            device_id=(lax.rem(beam_at + 1, SENDERS), freq_at),
            device_id_type=MESH,
        )

    block_rows = CHANNELS * OWN_BEAMS

    def spread_columns(first, last):
        rows_f32[first * block_rows : last * block_rows, :] = (
            incoming[first:last].astype(F32).reshape((last - first) * block_rows, SAMPLES)
        )
        for b in range(OWN_BEAMS):
            columns[first * CHANNELS : last * CHANNELS, b * SAMPLES : (b + 1) * SAMPLES] = rows_f32[
                pl.ds(first * block_rows + b, (last - first) * CHANNELS, stride=OWN_BEAMS), :
            ].astype(BF16)

    all_blocks(half_way, half_way).wait_recv()
    spread_columns(half_way, SENDERS)
    all_blocks(0, half_way).wait_recv()
    spread_columns(0, half_way)

    time = lax.broadcasted_iota(jnp.int32, (TRIALS, SAMPLES), 1)
    for pair in range(OWN_BEAMS // 2):
        spread = jnp.dot(
            selector[...], columns[:, pair * 2 * SAMPLES : (pair + 1) * 2 * SAMPLES], preferred_element_type=F32
        )
        for side in range(2):
            total = spread[:TRIALS, side * SAMPLES : (side + 1) * SAMPLES]
            for n in range(1, OFFSETS):
                piece = spread[n * TRIALS : (n + 1) * TRIALS, side * SAMPLES : (side + 1) * SAMPLES]
                total = total + jnp.where(time >= n, pltpu.roll(piece, n, 1), 0.0)
            b = 2 * pair + side
            partial_f32[b * TRIALS : (b + 1) * TRIALS, :] = total
    for r in range(TRIALS):
        window[0, r] = partial_f32[pl.ds(r, OWN_BEAMS, stride=TRIALS), :]
    own_block[...] = window[0].reshape(TRIALS * OWN_BEAMS, SAMPLES).astype(BF16)

    nears = []
    for slot, offset in enumerate(near_offsets):
        near = pltpu.make_async_remote_copy(
            src_ref=own_block,
            dst_ref=window_in.at[slot],
            send_sem=near_send.at[slot],
            recv_sem=near_recv.at[slot],
            device_id=(beam_at, ring(-offset)),
            device_id_type=MESH,
        )
        near.start()
        nears.append(near)

    def take_near(slot):
        nears[slot].wait_recv()
        window[slot + 1] = window_in[slot].astype(F32).reshape(TRIALS, OWN_BEAMS, SAMPLES)

    for slot in (2, 3, 0, 1):
        take_near(slot)

    to_scalars.wait()
    subbands = [freq_at] + [ring(offset) for offset in near_offsets]
    moment = lax.broadcasted_iota(jnp.int32, (OWN_BEAMS, SAMPLES), 1)

    def window_sum(to, k, places):
        total = None
        for place in range(places):
            entry = table[subbands[place], to * TRIALS + k]
            late = entry & 127
            moved = pltpu.roll(window[place, jnp.right_shift(entry, 7) & (TRIALS - 1)], late, 1)
            moved = jnp.where(moment >= late, moved, 0.0)
            total = moved if total is None else total + moved
        return total

    fars = []
    for slot, offset in enumerate(far_offsets):
        to = ring(-offset)

        def two_rows(n, carry, to=to, slot=slot):
            both = jnp.concatenate(
                [window_sum(to, 2 * n + side, PLACES - 1) for side in range(2)], axis=0
            )
            sums_out[slot, pl.ds(pl.multiple_of(n * 16, 16), 16), :] = both.astype(BF16)
            return carry

        lax.fori_loop(0, TRIALS // 2, two_rows, 0, unroll=4)
        far = pltpu.make_async_remote_copy(
            src_ref=sums_out.at[slot],
            dst_ref=sums_in.at[slot],
            send_sem=far_send.at[slot],
            recv_sem=far_recv.at[slot],
            device_id=(beam_at, to),
            device_id_type=MESH,
        )
        far.start()
        fars.append(far)

    take_near(NEARS - 1)

    def own_rows(k, carry):
        out_ref[k] = window_sum(freq_at, k, PLACES)
        return carry

    lax.fori_loop(0, TRIALS, own_rows, 0, unroll=8)

    all_blocks(0, SENDERS - 1).wait_send()
    for near in nears:
        near.wait_send()
    for far in fars:
        far.wait()
    gathered = sums_in[0].astype(F32) + sums_in[1].astype(F32)
    out_ref[...] = (out_ref[...] + gathered.reshape(TRIALS, OWN_BEAMS, SAMPLES)) * (1.0 / math.sqrt(2048.0))


def on_device(voltages, gains, channel_map, positions, directions, local_delay, merge_table):
    received = SENDERS * CHANNELS * OWN_BEAMS
    block = TRIALS * OWN_BEAMS
    return pl.pallas_call(
        kernel,
        out_shape=pltpu.VMEM((TRIALS, OWN_BEAMS, SAMPLES), F32),
        in_specs=[pl.BlockSpec(memory_space=pl.ANY)] * 7,
        out_specs=pl.BlockSpec(memory_space=pltpu.VMEM),
        scratch_shapes=[
            pltpu.VMEM((CHANNELS, 2, ANTENNAS), F32),
            pltpu.SMEM((CHANNELS,), jnp.int32),
            pltpu.VMEM((2, ANTENNAS), F32),
            pltpu.VMEM((2, BEAMS), F32),
            pltpu.VMEM((TRIALS, SENDERS * CHANNELS), jnp.int32),
            pltpu.VMEM((3, ENTRIES), jnp.int32),
            pltpu.VMEM((CHANNELS, ANTENNAS, 2 * SAMPLES), BF16),
            pltpu.VMEM((BEAMS, ANTENNAS), F32),
            pltpu.VMEM((2, BEAMS, 128), F32),
            pltpu.VMEM((CHANNELS, TURN_BEAMS, SAMPLES), F32),
            pltpu.VMEM((SENDERS, CHANNELS * OWN_BEAMS, SAMPLES), BF16),
            pltpu.VMEM((SENDERS, CHANNELS * OWN_BEAMS, SAMPLES), BF16),
            pltpu.VMEM((received + OWN_BEAMS, SAMPLES), F32),
            pltpu.VMEM((SENDERS * CHANNELS, OWN_BEAMS * SAMPLES), BF16),
            pltpu.VMEM((OFFSETS * TRIALS, SENDERS * CHANNELS), BF16),
            pltpu.VMEM((block + TRIALS, SAMPLES), F32),
            pltpu.VMEM((PLACES, TRIALS, OWN_BEAMS, SAMPLES), F32),
            pltpu.VMEM((block, SAMPLES), BF16),
            pltpu.VMEM((NEARS, block, SAMPLES), BF16),
            pltpu.VMEM((FARS, block, SAMPLES), BF16),
            pltpu.VMEM((FARS, block, SAMPLES), BF16),
            pltpu.VMEM((8, 512), jnp.int32),
            pltpu.VMEM((SUBBANDS, 256), jnp.int32),
            pltpu.SMEM((SUBBANDS, 256), jnp.int32),
            pltpu.SemaphoreType.DMA((6,)),
            pltpu.SemaphoreType.DMA((CHANNELS,)),
            pltpu.SemaphoreType.DMA,
            pltpu.SemaphoreType.DMA,
            pltpu.SemaphoreType.DMA((2,)),
            pltpu.SemaphoreType.DMA((NEARS,)),
            pltpu.SemaphoreType.DMA((NEARS,)),
            pltpu.SemaphoreType.DMA((FARS,)),
            pltpu.SemaphoreType.DMA((FARS,)),
        ],
        compiler_params=pltpu.CompilerParams(
            collective_id=0, has_side_effects=True, vmem_limit_bytes=48 * 2**20
        ),
        name="search_window",
    )(*[
        pltpu.with_memory_space_constraint(operand, pltpu.HBM)
        for operand in (voltages, gains, channel_map, positions, directions, local_delay, merge_table)
    ])


def solution(mesh):
    return jax.shard_map(
        on_device,
        mesh=mesh,
        in_specs=(
            P(("beam", "freq"), None, None),
            P(("beam", "freq"), None, None),
            P(("beam", "freq")),
            P(),
            P(),
            P("freq", None),
            P(),
        ),
        out_specs=P("freq", "beam", None),
        check_vma=False,
    )
```

```python
import functools
import math

import jax
import jax.numpy as jnp
from jax import lax
from jax.experimental import pallas as pl
from jax.experimental.pallas import tpu as pltpu
from jax.sharding import PartitionSpec as P

MESH = pl.DeviceIdType.MESH
F32 = jnp.float32
BF16 = jnp.bfloat16

CHANNELS = 4
ANTENNAS = 1024
BEAMS = 256
SAMPLES = 128
SENDERS = 32
GROUP = 8
GROUPS = SENDERS // GROUP
TURNS = 2
TURN_BEAMS = BEAMS // TURNS
TURN_SENDS = SENDERS // TURNS
OWN_BEAMS = BEAMS // SENDERS
TRIALS = 16
OFFSETS = 17
SUBBANDS = 16
REACH = 2
PLACES = 2 * REACH + 2
NEARS = PLACES - 1
FARS = 2
ENTRIES = 480
PART = 256
ORDER = (
    (2, 2), (1, 1), (3, 3), (0, 2), (2, 1), (1, 2), (3, 2), (0, 1),
    (2, 3), (1, 3), (3, 1), (0, 3), (2, 0), (1, 0), (3, 0), (0, 0),
)

SIN_TERMS = (2.22143036, -0.91317465, 0.10983828)
ROUNDER = 12582912.0


def horner(terms, z):
    total = z * terms[-1] + terms[-2]
    for term in terms[-3::-1]:
        total = total * z + term
    return total


def weight_pair(geometry, ratio, gain_re, gain_im):
    turns = geometry * ratio
    rest = turns - ((turns + ROUNDER) - ROUNDER)
    z = rest * rest
    quarter_sin = rest * horner(SIN_TERMS, z)
    square = quarter_sin * quarter_sin
    left = 2.0 - square
    half_sin = quarter_sin * (left * lax.rsqrt(left))
    half_cos = 1.0 - square
    doubled = half_sin + half_sin
    cosine = 1.0 - doubled * half_sin
    sine = doubled * half_cos
    return gain_re * cosine + gain_im * sine, gain_im * cosine - gain_re * sine


def kernel(
    volts_hbm, gains_hbm, channel_hbm, positions_hbm, directions_hbm, delay_hbm, merge_hbm, out_ref,
    gains_ref, channel_ref, positions_ref, directions_ref, delay_ref, merge_ref, volts, geometry, across, intensity, outgoing, incoming, rows_f32, columns,
    selector, partial_f32, window, own_block, window_in, sums_out, sums_in, table_pad, table_vmem, table,
    small_sem, volts_sem, table_sem, send_sem, recv_sem, near_send, near_recv, far_send, far_recv,
):
    beam_at = lax.axis_index("beam")
    freq_at = lax.axis_index("freq")
    row = beam_at // GROUP
    spot = lax.rem(beam_at // 2, GROUPS)
    core = lax.rem(beam_at, 2)
    lean = 1 - 2 * core

    def ring(offset):
        return lax.rem(freq_at + offset + SUBBANDS, SUBBANDS)

    def mate(distance, step, to_core):
        return lax.rem(row + distance, GROUPS) * GROUP + lax.rem(spot + step, GROUPS) * 2 + to_core

    smalls = [
        pltpu.make_async_copy(src, dst, small_sem.at[n])
        for n, (src, dst) in enumerate((
            (merge_hbm, merge_ref), (directions_hbm, directions_ref), (positions_hbm, positions_ref),
            (gains_hbm, gains_ref), (channel_hbm, channel_ref), (delay_hbm, delay_ref),
        ))
    ]
    for small in smalls:
        small.start()
    loads = [
        pltpu.make_async_copy(volts_hbm.at[c], volts.at[c], volts_sem.at[c]) for c in range(CHANNELS)
    ]
    for load in loads:
        load.start()

    barrier = pltpu.get_barrier_semaphore()

    for step in range(1, SENDERS):
        other = lax.rem(beam_at + step, SENDERS)
        pl.semaphore_signal(barrier, inc=1, device_id=(other, freq_at), device_id_type=MESH)
    near_offsets = (-2, 2, -1, 1, 3 * lean)
    far_offsets = (6 * lean, -5 * lean)
    for offset in near_offsets + far_offsets:
        pl.semaphore_signal(barrier, inc=1, device_id=(beam_at, ring(offset)), device_id_type=MESH)

    for small in smalls:
        small.wait()

    for k in range(2):
        across[k] = jnp.transpose(jnp.broadcast_to(directions_ref[k : k + 1, :], (128, BEAMS)))

    def geometry_rows(chip, carry):
        for to_core in range(2):
            at = pl.ds(pl.multiple_of(chip * 16 + to_core * 8, 8), 8)
            to = pl.ds(pl.multiple_of(to_core * (BEAMS // 2) + chip * 8, 8), 8)
            first, second = across[0, at, :], across[1, at, :]
            for n in range(ANTENNAS // 128):
                lanes = pl.ds(n * 128, 128)
                geometry[to, lanes] = (
                    first * positions_ref[0:1, lanes] + second * positions_ref[1:2, lanes]
                )
        return carry

    lax.fori_loop(0, SENDERS // 2, geometry_rows, 0)
    for load in loads:
        load.wait()

    def weights_of(to_core, c, part):
        lanes = pl.ds(part * PART, PART)
        ratio = 1.0 + channel_ref[c].astype(F32) * (1.0 / 2048.0)
        gain_re = jnp.broadcast_to(gains_ref[c, 0:1, lanes] * (1.0 / 32.0), (16, PART))
        gain_im = jnp.broadcast_to(gains_ref[c, 1:2, lanes] * (1.0 / 32.0), (16, PART))
        real, imag = [], []
        for n in range(TURN_BEAMS // 16):
            at = pl.ds(pl.multiple_of(to_core * (BEAMS // 2) + n * 16, 16), 16)
            pair = weight_pair(geometry[at, lanes], ratio, gain_re, gain_im)
            real.append(pair[0].astype(BF16))
            imag.append(pair[1].astype(BF16))
        return jnp.concatenate(real + imag, axis=0)

    def intensity_of(product):
        beam_re = product[:TURN_BEAMS, :SAMPLES] - product[TURN_BEAMS:, SAMPLES:]
        beam_im = product[:TURN_BEAMS, SAMPLES:] + product[TURN_BEAMS:, :SAMPLES]
        power = beam_re * beam_re + beam_im * beam_im
        mean = jnp.sum(power, axis=1, keepdims=True) * (1.0 / SAMPLES)
        return 0.25 * (power - mean)

    def shipment(distance, step, to_core, pair):
        to = mate(distance, step, to_core)
        tile = pl.ds(pair * 16, 16)
        return pltpu.make_async_remote_copy(
            src_ref=outgoing.at[to, tile],
            dst_ref=incoming.at[(distance * GROUPS + step) * 2 + core, tile],
            send_sem=send_sem,
            recv_sem=recv_sem.at[distance // 2],
            device_id=(to, freq_at),
            device_id_type=MESH,
        )

    def send_pair(to_core, pair):
        for n in range(TURN_SENDS):
            at = slice(n * OWN_BEAMS, (n + 1) * OWN_BEAMS)
            rows = jnp.concatenate([intensity[2 * pair + c, at, :] for c in range(2)], axis=0)
            outgoing[2 * n + to_core, pair * 16 : (pair + 1) * 16, :] = rows.astype(BF16)
        if pair == 0:

            @pl.when(to_core == 0)
            def _():
                pl.semaphore_wait(barrier, SENDERS - 1 + NEARS + FARS)

        for distance, step in ORDER[:-1]:
            shipment(distance, step, to_core, pair).start()

        @pl.when(to_core != core)
        def _():
            shipment(0, 0, to_core, pair).start()

    def beams_of(to_core):
        parts = [(c, part) for c in range(CHANNELS) for part in range(ANTENNAS // PART)]
        ready, product = weights_of(to_core, *parts[0]), None
        for n, (c, part) in enumerate(parts):
            following = weights_of(to_core, *parts[n + 1]) if n + 1 < len(parts) else None
            term = jnp.dot(ready, volts[c, pl.ds(part * PART, PART), :], preferred_element_type=F32)
            product = term if part == 0 else product + term
            if part + 1 == ANTENNAS // PART:
                intensity[c] = intensity_of(product)
                if c % 2 == 1:
                    send_pair(to_core, c // 2)
            ready = following

    def one_turn(to_core, carry):
        beams_of(to_core)
        return carry

    lax.fori_loop(0, TURNS, one_turn, 0)
    keep = pltpu.make_async_copy(outgoing.at[beam_at], incoming.at[core], recv_sem.at[0])
    keep.start()

    lane = lax.broadcasted_iota(jnp.int32, (8, 128), 1)
    channel = (
        ((row + GROUPS - jnp.right_shift(lane, 5)) & (GROUPS - 1)) * (GROUP * CHANNELS)
        + ((spot + GROUPS - (jnp.right_shift(lane, 3) & (GROUPS - 1))) & (GROUPS - 1)) * (2 * CHANNELS)
        + (jnp.right_shift(lane, 2) & 1) * CHANNELS
        + (lane & (CHANNELS - 1))
    )
    delays = jnp.concatenate(
        [
            jnp.take_along_axis(delay_ref[8 * n : 8 * n + 8, :], channel, axis=1, mode="promise_in_bounds")
            for n in range(TRIALS // 8)
        ],
        axis=0,
    )
    selector[...] = jnp.concatenate(
        [jnp.where(delays == n, 1.0, 0.0) for n in range(OFFSETS)], axis=0
    ).astype(BF16)

    half_way = SENDERS // 2

    def all_blocks(first, count):
        return pltpu.make_async_remote_copy(
            src_ref=outgoing.at[pl.ds(first, count)],
            dst_ref=incoming.at[pl.ds(first, count)],
            send_sem=send_sem,
            recv_sem=recv_sem.at[first // half_way],
            device_id=(lax.rem(beam_at + 1, SENDERS), freq_at),
            device_id_type=MESH,
        )

    block_rows = CHANNELS * OWN_BEAMS

    def spread_columns(first, last):
        rows_f32[first * block_rows : last * block_rows, :] = (
            incoming[first:last].astype(F32).reshape((last - first) * block_rows, SAMPLES)
        )
        for b in range(OWN_BEAMS):
            columns[first * CHANNELS : last * CHANNELS, b * SAMPLES : (b + 1) * SAMPLES] = rows_f32[
                pl.ds(first * block_rows + b, (last - first) * CHANNELS, stride=OWN_BEAMS), :
            ].astype(BF16)

    all_blocks(half_way, half_way).wait_recv()
    spread_columns(half_way, SENDERS)
    all_blocks(0, half_way).wait_recv()
    spread_columns(0, half_way)

    time = lax.broadcasted_iota(jnp.int32, (TRIALS, SAMPLES), 1)
    for pair in range(OWN_BEAMS // 2):
        spread = jnp.dot(
            selector[...], columns[:, pair * 2 * SAMPLES : (pair + 1) * 2 * SAMPLES], preferred_element_type=F32
        )
        for side in range(2):
            total = spread[:TRIALS, side * SAMPLES : (side + 1) * SAMPLES]
            for n in range(1, OFFSETS):
                piece = spread[n * TRIALS : (n + 1) * TRIALS, side * SAMPLES : (side + 1) * SAMPLES]
                total = total + jnp.where(time >= n, pltpu.roll(piece, n, 1), 0.0)
            b = 2 * pair + side
            partial_f32[b * TRIALS : (b + 1) * TRIALS, :] = total
    for r in range(TRIALS):
        window[0, r] = partial_f32[pl.ds(r, OWN_BEAMS, stride=TRIALS), :]
    own_block[...] = window[0].reshape(TRIALS * OWN_BEAMS, SAMPLES).astype(BF16)

    nears = []
    for slot, offset in enumerate(near_offsets):
        near = pltpu.make_async_remote_copy(
            src_ref=own_block,
            dst_ref=window_in.at[slot],
            send_sem=near_send.at[slot],
            recv_sem=near_recv.at[slot],
            device_id=(beam_at, ring(-offset)),
            device_id_type=MESH,
        )
        near.start()
        nears.append(near)

    table_pad[...] = jnp.zeros_like(table_pad)
    table_pad[0:3, 0:ENTRIES] = merge_ref[...]
    code = table_pad[0:1, :] + 128 * table_pad[1:2, :] + 16384 * table_pad[2:3, :]
    pieces = [jnp.broadcast_to(code[:, 128 * n : 128 * (n + 1)], (8, 128)) for n in range(4)]
    turned = [pltpu.roll(piece, 32, 1) for piece in pieces]
    level_zero = pieces[0]
    level_one = pltpu.roll(pieces[0], 96, 1)
    level_two = jnp.where(lane < 32, turned[0], turned[1])
    last = [jnp.where(lane < 32, turned[1], turned[2]), jnp.where(lane < 32, turned[2], turned[3])]
    for part in range(2):
        subband = part * 8 + lax.broadcasted_iota(jnp.int32, (8, 128), 0)
        for half in range(2):
            found = last[half]
            late = jnp.zeros((8, 128), jnp.int32)
            for bit, level in ((3, level_two), (2, level_one), (1, level_zero), (0, None)):
                upper = lax.rem(jnp.right_shift(subband, bit), 2) == 1
                at = jnp.where(upper, jnp.right_shift(found, 7), found) & 127
                late = late + jnp.where(upper, jnp.right_shift(found, 14), 0)
                if level is not None:
                    found = jnp.take_along_axis(level, at, axis=1, mode="promise_in_bounds")
            table_vmem[pl.ds(part * 8, 8), pl.ds(half * 128, 128)] = at * 128 + late
    to_scalars = pltpu.make_async_copy(table_vmem, table, table_sem)
    to_scalars.start()

    def take_near(slot):
        nears[slot].wait_recv()
        window[slot + 1] = window_in[slot].astype(F32).reshape(TRIALS, OWN_BEAMS, SAMPLES)

    for slot in (2, 3, 0, 1):
        take_near(slot)

    to_scalars.wait()
    subbands = [freq_at] + [ring(offset) for offset in near_offsets]
    moment = lax.broadcasted_iota(jnp.int32, (OWN_BEAMS, SAMPLES), 1)

    def window_sum(to, k, places):
        total = None
        for place in range(places):
            entry = table[subbands[place], to * TRIALS + k]
            late = entry & 127
            moved = pltpu.roll(window[place, jnp.right_shift(entry, 7) & (TRIALS - 1)], late, 1)
            moved = jnp.where(moment >= late, moved, 0.0)
            total = moved if total is None else total + moved
        return total

    fars = []
    for slot, offset in enumerate(far_offsets):
        to = ring(-offset)

        def two_rows(n, carry, to=to, slot=slot):
            both = jnp.concatenate(
                [window_sum(to, 2 * n + side, PLACES - 1) for side in range(2)], axis=0
            )
            sums_out[slot, pl.ds(pl.multiple_of(n * 16, 16), 16), :] = both.astype(BF16)
            return carry

        lax.fori_loop(0, TRIALS // 2, two_rows, 0, unroll=4)
        far = pltpu.make_async_remote_copy(
            src_ref=sums_out.at[slot],
            dst_ref=sums_in.at[slot],
            send_sem=far_send.at[slot],
            recv_sem=far_recv.at[slot],
            device_id=(beam_at, to),
            device_id_type=MESH,
        )
        far.start()
        fars.append(far)

    take_near(NEARS - 1)

    def own_rows(k, carry):
        out_ref[k] = window_sum(freq_at, k, PLACES)
        return carry

    lax.fori_loop(0, TRIALS, own_rows, 0, unroll=8)

    all_blocks(0, SENDERS - 1).wait_send()
    for near in nears:
        near.wait_send()
    for far in fars:
        far.wait()
    gathered = sums_in[0].astype(F32) + sums_in[1].astype(F32)
    out_ref[...] = (out_ref[...] + gathered.reshape(TRIALS, OWN_BEAMS, SAMPLES)) * (1.0 / math.sqrt(2048.0))


def on_device(voltages, gains, channel_map, positions, directions, local_delay, merge_table):
    received = SENDERS * CHANNELS * OWN_BEAMS
    block = TRIALS * OWN_BEAMS
    return pl.pallas_call(
        kernel,
        out_shape=pltpu.VMEM((TRIALS, OWN_BEAMS, SAMPLES), F32),
        in_specs=[pl.BlockSpec(memory_space=pl.ANY)] * 7,
        out_specs=pl.BlockSpec(memory_space=pltpu.VMEM),
        scratch_shapes=[
            pltpu.VMEM((CHANNELS, 2, ANTENNAS), F32),
            pltpu.SMEM((CHANNELS,), jnp.int32),
            pltpu.VMEM((2, ANTENNAS), F32),
            pltpu.VMEM((2, BEAMS), F32),
            pltpu.VMEM((TRIALS, SENDERS * CHANNELS), jnp.int32),
            pltpu.VMEM((3, ENTRIES), jnp.int32),
            pltpu.VMEM((CHANNELS, ANTENNAS, 2 * SAMPLES), BF16),
            pltpu.VMEM((BEAMS, ANTENNAS), F32),
            pltpu.VMEM((2, BEAMS, 128), F32),
            pltpu.VMEM((CHANNELS, TURN_BEAMS, SAMPLES), F32),
            pltpu.VMEM((SENDERS, CHANNELS * OWN_BEAMS, SAMPLES), BF16),
            pltpu.VMEM((SENDERS, CHANNELS * OWN_BEAMS, SAMPLES), BF16),
            pltpu.VMEM((received + OWN_BEAMS, SAMPLES), F32),
            pltpu.VMEM((SENDERS * CHANNELS, OWN_BEAMS * SAMPLES), BF16),
            pltpu.VMEM((OFFSETS * TRIALS, SENDERS * CHANNELS), BF16),
            pltpu.VMEM((block + TRIALS, SAMPLES), F32),
            pltpu.VMEM((PLACES, TRIALS, OWN_BEAMS, SAMPLES), F32),
            pltpu.VMEM((block, SAMPLES), BF16),
            pltpu.VMEM((NEARS, block, SAMPLES), BF16),
            pltpu.VMEM((FARS, block, SAMPLES), BF16),
            pltpu.VMEM((FARS, block, SAMPLES), BF16),
            pltpu.VMEM((8, 512), jnp.int32),
            pltpu.VMEM((SUBBANDS, 256), jnp.int32),
            pltpu.SMEM((SUBBANDS, 256), jnp.int32),
            pltpu.SemaphoreType.DMA((6,)),
            pltpu.SemaphoreType.DMA((CHANNELS,)),
            pltpu.SemaphoreType.DMA,
            pltpu.SemaphoreType.DMA,
            pltpu.SemaphoreType.DMA((2,)),
            pltpu.SemaphoreType.DMA((NEARS,)),
            pltpu.SemaphoreType.DMA((NEARS,)),
            pltpu.SemaphoreType.DMA((FARS,)),
            pltpu.SemaphoreType.DMA((FARS,)),
        ],
        compiler_params=pltpu.CompilerParams(
            collective_id=0, has_side_effects=True, vmem_limit_bytes=48 * 2**20
        ),
        name="search_window",
    )(*[
        pltpu.with_memory_space_constraint(operand, pltpu.HBM)
        for operand in (voltages, gains, channel_map, positions, directions, local_delay, merge_table)
    ])


def solution(mesh):
    return jax.shard_map(
        on_device,
        mesh=mesh,
        in_specs=(
            P(("beam", "freq"), None, None),
            P(("beam", "freq"), None, None),
            P(("beam", "freq")),
            P(),
            P(),
            P("freq", None),
            P(),
        ),
        out_specs=P("freq", "beam", None),
        check_vma=False,
    )
```

```python
import functools
import math

import jax
import jax.numpy as jnp
from jax import lax
from jax.experimental import pallas as pl
from jax.experimental.pallas import tpu as pltpu
from jax.sharding import PartitionSpec as P

MESH = pl.DeviceIdType.MESH
F32 = jnp.float32
BF16 = jnp.bfloat16

CHANNELS = 4
ANTENNAS = 1024
BEAMS = 256
SAMPLES = 128
SENDERS = 32
GROUP = 8
GROUPS = SENDERS // GROUP
TURNS = 2
TURN_BEAMS = BEAMS // TURNS
TURN_SENDS = SENDERS // TURNS
OWN_BEAMS = BEAMS // SENDERS
TRIALS = 16
OFFSETS = 17
SUBBANDS = 16
REACH = 2
PLACES = 2 * REACH + 2
NEARS = PLACES - 1
FARS = 2
ENTRIES = 480
PART = 256
ORDER = (
    (2, 2), (1, 1), (3, 3), (0, 2), (2, 1), (1, 2), (3, 2), (0, 1),
    (2, 3), (1, 3), (3, 1), (0, 3), (2, 0), (1, 0), (3, 0), (0, 0),
)

SIN_TERMS = (2.22143036, -0.91317465, 0.10983828)
ROUNDER = 12582912.0


def horner(terms, z):
    total = z * terms[-1] + terms[-2]
    for term in terms[-3::-1]:
        total = total * z + term
    return total


def weight_pair(geometry, ratio, gain_re, gain_im):
    turns = geometry * ratio
    rest = turns - ((turns + ROUNDER) - ROUNDER)
    z = rest * rest
    quarter_sin = rest * horner(SIN_TERMS, z)
    square = quarter_sin * quarter_sin
    left = 2.0 - square
    half_sin = quarter_sin * (left * lax.rsqrt(left))
    half_cos = 1.0 - square
    doubled = half_sin + half_sin
    cosine = 1.0 - doubled * half_sin
    sine = doubled * half_cos
    return gain_re * cosine + gain_im * sine, gain_im * cosine - gain_re * sine


def kernel(
    volts_hbm, gains_hbm, channel_hbm, positions_hbm, directions_hbm, delay_hbm, merge_hbm, out_ref,
    gains_ref, channel_ref, positions_ref, directions_ref, delay_ref, merge_ref, volts, geometry, across, intensity, outgoing, incoming, rows_f32, columns,
    selector, partial_f32, window, own_block, window_in, sums_out, sums_in, early, table_pad, table_vmem, table,
    small_sem, volts_sem, table_sem, send_sem, recv_sem, near_send, near_recv, far_send, far_recv,
):
    beam_at = lax.axis_index("beam")
    freq_at = lax.axis_index("freq")
    row = beam_at // GROUP
    spot = lax.rem(beam_at // 2, GROUPS)
    core = lax.rem(beam_at, 2)
    lean = 1 - 2 * core

    def ring(offset):
        return lax.rem(freq_at + offset + SUBBANDS, SUBBANDS)

    def mate(distance, step, to_core):
        return lax.rem(row + distance, GROUPS) * GROUP + lax.rem(spot + step, GROUPS) * 2 + to_core

    smalls = [
        pltpu.make_async_copy(src, dst, small_sem.at[n])
        for n, (src, dst) in enumerate((
            (merge_hbm, merge_ref), (directions_hbm, directions_ref), (positions_hbm, positions_ref),
            (gains_hbm, gains_ref), (channel_hbm, channel_ref), (delay_hbm, delay_ref),
        ))
    ]
    for small in smalls:
        small.start()
    loads = [
        pltpu.make_async_copy(volts_hbm.at[c], volts.at[c], volts_sem.at[c]) for c in range(CHANNELS)
    ]
    for load in loads:
        load.start()

    barrier = pltpu.get_barrier_semaphore()

    for step in range(1, SENDERS):
        other = lax.rem(beam_at + step, SENDERS)
        pl.semaphore_signal(barrier, inc=1, device_id=(other, freq_at), device_id_type=MESH)
    near_offsets = (-1, 1, -2, 2, 3 * lean)
    far_offsets = (6 * lean, -5 * lean)
    for offset in near_offsets + far_offsets:
        pl.semaphore_signal(barrier, inc=1, device_id=(beam_at, ring(offset)), device_id_type=MESH)

    for small in smalls:
        small.wait()

    for k in range(2):
        across[k] = jnp.transpose(jnp.broadcast_to(directions_ref[k : k + 1, :], (128, BEAMS)))

    def geometry_rows(chip, carry):
        for to_core in range(2):
            at = pl.ds(pl.multiple_of(chip * 16 + to_core * 8, 8), 8)
            to = pl.ds(pl.multiple_of(to_core * (BEAMS // 2) + chip * 8, 8), 8)
            first, second = across[0, at, :], across[1, at, :]
            for n in range(ANTENNAS // 128):
                lanes = pl.ds(n * 128, 128)
                geometry[to, lanes] = (
                    first * positions_ref[0:1, lanes] + second * positions_ref[1:2, lanes]
                )
        return carry

    lax.fori_loop(0, SENDERS // 2, geometry_rows, 0)
    for load in loads:
        load.wait()

    def weights_of(to_core, c, part):
        lanes = pl.ds(part * PART, PART)
        ratio = 1.0 + channel_ref[c].astype(F32) * (1.0 / 2048.0)
        gain_re = jnp.broadcast_to(gains_ref[c, 0:1, lanes] * (1.0 / 32.0), (16, PART))
        gain_im = jnp.broadcast_to(gains_ref[c, 1:2, lanes] * (1.0 / 32.0), (16, PART))
        real, imag = [], []
        for n in range(TURN_BEAMS // 16):
            at = pl.ds(pl.multiple_of(to_core * (BEAMS // 2) + n * 16, 16), 16)
            pair = weight_pair(geometry[at, lanes], ratio, gain_re, gain_im)
            real.append(pair[0].astype(BF16))
            imag.append(pair[1].astype(BF16))
        return jnp.concatenate(real + imag, axis=0)

    def intensity_of(product):
        beam_re = product[:TURN_BEAMS, :SAMPLES] - product[TURN_BEAMS:, SAMPLES:]
        beam_im = product[:TURN_BEAMS, SAMPLES:] + product[TURN_BEAMS:, :SAMPLES]
        power = beam_re * beam_re + beam_im * beam_im
        mean = jnp.sum(power, axis=1, keepdims=True) * (1.0 / SAMPLES)
        return 0.25 * (power - mean)

    def beams_of(to_core):
        parts = [(c, part) for c in range(CHANNELS) for part in range(ANTENNAS // PART)]
        ready, product = weights_of(to_core, *parts[0]), None
        for n, (c, part) in enumerate(parts):
            following = weights_of(to_core, *parts[n + 1]) if n + 1 < len(parts) else None
            term = jnp.dot(ready, volts[c, pl.ds(part * PART, PART), :], preferred_element_type=F32)
            product = term if part == 0 else product + term
            if part + 1 == ANTENNAS // PART:
                intensity[c] = intensity_of(product)
            ready = following
        for n in range(TURN_SENDS):
            for pair in range(CHANNELS // 2):
                rows = jnp.concatenate(
                    [intensity[2 * pair + c, n * OWN_BEAMS : (n + 1) * OWN_BEAMS, :] for c in range(2)], axis=0
                )
                outgoing[2 * n + to_core, pair * 16 : (pair + 1) * 16, :] = rows.astype(BF16)

    def shipment(distance, step, to_core):
        to = mate(distance, step, to_core)
        slot = (distance * GROUPS + step) * 2 + core
        return pltpu.make_async_remote_copy(
            src_ref=outgoing.at[to],
            dst_ref=incoming.at[slot],
            send_sem=send_sem,
            recv_sem=recv_sem.at[distance // 2],
            device_id=(to, freq_at),
            device_id_type=MESH,
        )

    def beams_and_send(to_core, carry):
        beams_of(to_core)

        @pl.when(to_core == 0)
        def _():
            pl.semaphore_wait(barrier, SENDERS - 1 + NEARS + FARS)

        for distance, step in ORDER[:-1]:
            shipment(distance, step, to_core).start()

        @pl.when(to_core != core)
        def _():
            shipment(0, 0, to_core).start()

        return carry

    lax.fori_loop(0, TURNS, beams_and_send, 0)
    keep = pltpu.make_async_copy(outgoing.at[beam_at], incoming.at[core], recv_sem.at[0])
    keep.start()

    lane = lax.broadcasted_iota(jnp.int32, (8, 128), 1)
    channel = (
        ((row + GROUPS - jnp.right_shift(lane, 5)) & (GROUPS - 1)) * (GROUP * CHANNELS)
        + ((spot + GROUPS - (jnp.right_shift(lane, 3) & (GROUPS - 1))) & (GROUPS - 1)) * (2 * CHANNELS)
        + (jnp.right_shift(lane, 2) & 1) * CHANNELS
        + (lane & (CHANNELS - 1))
    )
    delays = jnp.concatenate(
        [
            jnp.take_along_axis(delay_ref[8 * n : 8 * n + 8, :], channel, axis=1, mode="promise_in_bounds")
            for n in range(TRIALS // 8)
        ],
        axis=0,
    )
    selector[...] = jnp.concatenate(
        [jnp.where(delays == n, 1.0, 0.0) for n in range(OFFSETS)], axis=0
    ).astype(BF16)

    half_way = SENDERS // 2

    def all_blocks(first, count):
        return pltpu.make_async_remote_copy(
            src_ref=outgoing.at[pl.ds(first, count)],
            dst_ref=incoming.at[pl.ds(first, count)],
            send_sem=send_sem,
            recv_sem=recv_sem.at[first // half_way],
            device_id=(lax.rem(beam_at + 1, SENDERS), freq_at),
            device_id_type=MESH,
        )

    block_rows = CHANNELS * OWN_BEAMS

    def spread_columns(first, last):
        rows_f32[first * block_rows : last * block_rows, :] = (
            incoming[first:last].astype(F32).reshape((last - first) * block_rows, SAMPLES)
        )
        for b in range(OWN_BEAMS):
            columns[first * CHANNELS : last * CHANNELS, b * SAMPLES : (b + 1) * SAMPLES] = rows_f32[
                pl.ds(first * block_rows + b, (last - first) * CHANNELS, stride=OWN_BEAMS), :
            ].astype(BF16)

    all_blocks(half_way, half_way).wait_recv()
    spread_columns(half_way, SENDERS)
    all_blocks(0, half_way).wait_recv()
    spread_columns(0, half_way)

    time = lax.broadcasted_iota(jnp.int32, (TRIALS, SAMPLES), 1)
    for pair in range(OWN_BEAMS // 2):
        spread = jnp.dot(
            selector[...], columns[:, pair * 2 * SAMPLES : (pair + 1) * 2 * SAMPLES], preferred_element_type=F32
        )
        for side in range(2):
            total = spread[:TRIALS, side * SAMPLES : (side + 1) * SAMPLES]
            for n in range(1, OFFSETS):
                piece = spread[n * TRIALS : (n + 1) * TRIALS, side * SAMPLES : (side + 1) * SAMPLES]
                total = total + jnp.where(time >= n, pltpu.roll(piece, n, 1), 0.0)
            b = 2 * pair + side
            partial_f32[b * TRIALS : (b + 1) * TRIALS, :] = total
    for r in range(TRIALS):
        window[0, r] = partial_f32[pl.ds(r, OWN_BEAMS, stride=TRIALS), :]
    own_block[...] = window[0].reshape(TRIALS * OWN_BEAMS, SAMPLES).astype(BF16)

    nears = []
    for slot, offset in enumerate(near_offsets):
        near = pltpu.make_async_remote_copy(
            src_ref=own_block,
            dst_ref=window_in.at[slot],
            send_sem=near_send.at[slot],
            recv_sem=near_recv.at[slot],
            device_id=(beam_at, ring(-offset)),
            device_id_type=MESH,
        )
        near.start()
        nears.append(near)

    table_pad[...] = jnp.zeros_like(table_pad)
    table_pad[0:3, 0:ENTRIES] = merge_ref[...]
    code = table_pad[0:1, :] + 128 * table_pad[1:2, :] + 16384 * table_pad[2:3, :]
    pieces = [jnp.broadcast_to(code[:, 128 * n : 128 * (n + 1)], (8, 128)) for n in range(4)]
    turned = [pltpu.roll(piece, 32, 1) for piece in pieces]
    level_zero = pieces[0]
    level_one = pltpu.roll(pieces[0], 96, 1)
    level_two = jnp.where(lane < 32, turned[0], turned[1])
    last = [jnp.where(lane < 32, turned[1], turned[2]), jnp.where(lane < 32, turned[2], turned[3])]
    for part in range(2):
        subband = part * 8 + lax.broadcasted_iota(jnp.int32, (8, 128), 0)
        for half in range(2):
            found = last[half]
            late = jnp.zeros((8, 128), jnp.int32)
            for bit, level in ((3, level_two), (2, level_one), (1, level_zero), (0, None)):
                upper = lax.rem(jnp.right_shift(subband, bit), 2) == 1
                at = jnp.where(upper, jnp.right_shift(found, 7), found) & 127
                late = late + jnp.where(upper, jnp.right_shift(found, 14), 0)
                if level is not None:
                    found = jnp.take_along_axis(level, at, axis=1, mode="promise_in_bounds")
            table_vmem[pl.ds(part * 8, 8), pl.ds(half * 128, 128)] = at * 128 + late
    to_scalars = pltpu.make_async_copy(table_vmem, table, table_sem)
    to_scalars.start()

    def take_near(slot):
        nears[slot].wait_recv()
        window[slot + 1] = window_in[slot].astype(F32).reshape(TRIALS, OWN_BEAMS, SAMPLES)

    to_scalars.wait()
    take_near(0)
    take_near(1)
    subbands = [freq_at] + [ring(offset) for offset in near_offsets]
    moment = lax.broadcasted_iota(jnp.int32, (OWN_BEAMS, SAMPLES), 1)

    def window_sum(to, k, places):
        total = None
        for place in places:
            entry = table[subbands[place], to * TRIALS + k]
            late = entry & 127
            moved = pltpu.roll(window[place, jnp.right_shift(entry, 7) & (TRIALS - 1)], late, 1)
            moved = jnp.where(moment >= late, moved, 0.0)
            total = moved if total is None else total + moved
        return total

    far_to = [ring(-offset) for offset in far_offsets]

    def early_rows(k, carry):
        for f in range(FARS):
            early[f, k] = window_sum(far_to[f], k, (0, 1, 2))
        return carry

    lax.fori_loop(0, TRIALS, early_rows, 0, unroll=4)
    take_near(2)
    take_near(3)

    fars = []
    for f in range(FARS):

        def two_rows(n, carry, f=f):
            both = [early[f, k] + window_sum(far_to[f], k, (3, 4)) for k in (2 * n, 2 * n + 1)]
            sums_out[f, pl.ds(pl.multiple_of(n * 16, 16), 16), :] = jnp.concatenate(both, axis=0).astype(BF16)
            return carry

        lax.fori_loop(0, TRIALS // 2, two_rows, 0, unroll=True)
        far = pltpu.make_async_remote_copy(
            src_ref=sums_out.at[f],
            dst_ref=sums_in.at[f],
            send_sem=far_send.at[f],
            recv_sem=far_recv.at[f],
            device_id=(beam_at, far_to[f]),
            device_id_type=MESH,
        )
        far.start()
        fars.append(far)

    take_near(NEARS - 1)

    def own_rows(k, carry):
        out_ref[k] = window_sum(freq_at, k, range(PLACES))
        return carry

    lax.fori_loop(0, TRIALS, own_rows, 0, unroll=8)

    all_blocks(0, SENDERS - 1).wait_send()
    for near in nears:
        near.wait_send()
    for far in fars:
        far.wait()
    gathered = sums_in[0].astype(F32) + sums_in[1].astype(F32)
    out_ref[...] = (out_ref[...] + gathered.reshape(TRIALS, OWN_BEAMS, SAMPLES)) * (1.0 / math.sqrt(2048.0))


def on_device(voltages, gains, channel_map, positions, directions, local_delay, merge_table):
    received = SENDERS * CHANNELS * OWN_BEAMS
    block = TRIALS * OWN_BEAMS
    return pl.pallas_call(
        kernel,
        out_shape=pltpu.VMEM((TRIALS, OWN_BEAMS, SAMPLES), F32),
        in_specs=[pl.BlockSpec(memory_space=pl.ANY)] * 7,
        out_specs=pl.BlockSpec(memory_space=pltpu.VMEM),
        scratch_shapes=[
            pltpu.VMEM((CHANNELS, 2, ANTENNAS), F32),
            pltpu.SMEM((CHANNELS,), jnp.int32),
            pltpu.VMEM((2, ANTENNAS), F32),
            pltpu.VMEM((2, BEAMS), F32),
            pltpu.VMEM((TRIALS, SENDERS * CHANNELS), jnp.int32),
            pltpu.VMEM((3, ENTRIES), jnp.int32),
            pltpu.VMEM((CHANNELS, ANTENNAS, 2 * SAMPLES), BF16),
            pltpu.VMEM((BEAMS, ANTENNAS), F32),
            pltpu.VMEM((2, BEAMS, 128), F32),
            pltpu.VMEM((CHANNELS, TURN_BEAMS, SAMPLES), F32),
            pltpu.VMEM((SENDERS, CHANNELS * OWN_BEAMS, SAMPLES), BF16),
            pltpu.VMEM((SENDERS, CHANNELS * OWN_BEAMS, SAMPLES), BF16),
            pltpu.VMEM((received + OWN_BEAMS, SAMPLES), F32),
            pltpu.VMEM((SENDERS * CHANNELS, OWN_BEAMS * SAMPLES), BF16),
            pltpu.VMEM((OFFSETS * TRIALS, SENDERS * CHANNELS), BF16),
            pltpu.VMEM((block + TRIALS, SAMPLES), F32),
            pltpu.VMEM((PLACES, TRIALS, OWN_BEAMS, SAMPLES), F32),
            pltpu.VMEM((block, SAMPLES), BF16),
            pltpu.VMEM((NEARS, block, SAMPLES), BF16),
            pltpu.VMEM((FARS, block, SAMPLES), BF16),
            pltpu.VMEM((FARS, block, SAMPLES), BF16),
            pltpu.VMEM((FARS, TRIALS, OWN_BEAMS, SAMPLES), F32),
            pltpu.VMEM((8, 512), jnp.int32),
            pltpu.VMEM((SUBBANDS, 256), jnp.int32),
            pltpu.SMEM((SUBBANDS, 256), jnp.int32),
            pltpu.SemaphoreType.DMA((6,)),
            pltpu.SemaphoreType.DMA((CHANNELS,)),
            pltpu.SemaphoreType.DMA,
            pltpu.SemaphoreType.DMA,
            pltpu.SemaphoreType.DMA((2,)),
            pltpu.SemaphoreType.DMA((NEARS,)),
            pltpu.SemaphoreType.DMA((NEARS,)),
            pltpu.SemaphoreType.DMA((FARS,)),
            pltpu.SemaphoreType.DMA((FARS,)),
        ],
        compiler_params=pltpu.CompilerParams(
            collective_id=0, has_side_effects=True, vmem_limit_bytes=48 * 2**20
        ),
        name="search_window",
    )(*[
        pltpu.with_memory_space_constraint(operand, pltpu.HBM)
        for operand in (voltages, gains, channel_map, positions, directions, local_delay, merge_table)
    ])


def solution(mesh):
    return jax.shard_map(
        on_device,
        mesh=mesh,
        in_specs=(
            P(("beam", "freq"), None, None),
            P(("beam", "freq"), None, None),
            P(("beam", "freq")),
            P(),
            P(),
            P("freq", None),
            P(),
        ),
        out_specs=P("freq", "beam", None),
        check_vma=False,
    )
```

```python
import functools
import math

import jax
import jax.numpy as jnp
from jax import lax
from jax.experimental import pallas as pl
from jax.experimental.pallas import tpu as pltpu
from jax.sharding import PartitionSpec as P

MESH = pl.DeviceIdType.MESH
F32 = jnp.float32
BF16 = jnp.bfloat16

CHANNELS = 4
ANTENNAS = 1024
BEAMS = 256
SAMPLES = 128
SENDERS = 32
GROUP = 8
GROUPS = SENDERS // GROUP
TURNS = 2
TURN_BEAMS = BEAMS // TURNS
TURN_SENDS = SENDERS // TURNS
OWN_BEAMS = BEAMS // SENDERS
TRIALS = 16
OFFSETS = 17
SUBBANDS = 16
REACH = 2
PLACES = 2 * REACH + 2
NEARS = PLACES - 1
FARS = 2
ENTRIES = 480
PART = 512
ORDER = (
    (2, 2), (3, 3), (2, 1), (3, 2), (2, 3), (3, 1), (2, 0), (3, 0),
    (1, 1), (0, 2), (1, 2), (0, 1), (1, 3), (0, 3), (1, 0), (0, 0),
)

SIN_TERMS = (2.641740790, -1.085953791, 0.130620464)
ROOT_TWO = math.sqrt(2.0)
ROUNDER = 12582912.0


def horner(terms, z):
    total = z * terms[-1] + terms[-2]
    for term in terms[-3::-1]:
        total = total * z + term
    return total


def weight_pair(geometry, ratio, gain_re, gain_im):
    turns = geometry * ratio
    rest = turns - ((turns + ROUNDER) - ROUNDER)
    z = rest * rest
    quarter_sin = rest * horner(SIN_TERMS, z)
    square = quarter_sin * quarter_sin
    left = 2.0 * ROOT_TWO - square
    half_sin = quarter_sin * (left * lax.rsqrt(left))
    cosine = 1.0 - half_sin * half_sin
    sine = half_sin * (ROOT_TWO - square)
    return gain_re * cosine + gain_im * sine, gain_im * cosine - gain_re * sine


def kernel(
    volts_hbm, gains_hbm, channel_hbm, positions_hbm, directions_hbm, delay_hbm, merge_hbm, out_ref,
    gains_ref, channel_ref, positions_ref, directions_ref, delay_ref, merge_ref, volts, geometry, across, intensity, outgoing, incoming, rows_f32, columns,
    selector, partial_f32, window, own_block, window_in, sums_out, sums_in, early, table_pad, table_vmem, table,
    small_sem, volts_sem, table_sem, send_sem, recv_sem, near_send, near_recv, far_send, far_recv,
):
    beam_at = lax.axis_index("beam")
    freq_at = lax.axis_index("freq")
    row = beam_at // GROUP
    spot = lax.rem(beam_at // 2, GROUPS)
    core = lax.rem(beam_at, 2)
    lean = 1 - 2 * core

    def ring(offset):
        return lax.rem(freq_at + offset + SUBBANDS, SUBBANDS)

    def mate(distance, step, to_core):
        return lax.rem(row + distance, GROUPS) * GROUP + lax.rem(spot + step, GROUPS) * 2 + to_core

    smalls = [
        pltpu.make_async_copy(src, dst, small_sem.at[n])
        for n, (src, dst) in enumerate((
            (directions_hbm, directions_ref), (positions_hbm, positions_ref), (gains_hbm, gains_ref),
            (channel_hbm, channel_ref), (delay_hbm, delay_ref), (merge_hbm, merge_ref),
        ))
    ]
    for small in smalls:
        small.start()
    load = pltpu.make_async_copy(volts_hbm, volts, volts_sem)
    load.start()

    barrier = pltpu.get_barrier_semaphore()

    for step in range(1, SENDERS):
        other = lax.rem(beam_at + step, SENDERS)
        pl.semaphore_signal(barrier, inc=1, device_id=(other, freq_at), device_id_type=MESH)
    near_offsets = (-1, 1, -2, 2, 3 * lean)
    far_offsets = (6 * lean, -5 * lean)
    for offset in near_offsets + far_offsets:
        pl.semaphore_signal(barrier, inc=1, device_id=(beam_at, ring(offset)), device_id_type=MESH)

    for small in smalls[:2]:
        small.wait()

    for k in range(2):
        across[k] = jnp.transpose(jnp.broadcast_to(directions_ref[k : k + 1, :], (128, BEAMS)))

    def geometry_rows(chip, carry):
        for to_core in range(2):
            at = pl.ds(pl.multiple_of(chip * 16 + to_core * 8, 8), 8)
            to = pl.ds(pl.multiple_of(to_core * (BEAMS // 2) + chip * 8, 8), 8)
            first, second = across[0, at, :], across[1, at, :]
            for n in range(ANTENNAS // 128):
                lanes = pl.ds(n * 128, 128)
                geometry[to, lanes] = (
                    first * positions_ref[0:1, lanes] + second * positions_ref[1:2, lanes]
                )
        return carry

    lax.fori_loop(0, SENDERS // 2, geometry_rows, 0)
    for small in smalls[2:]:
        small.wait()
    load.wait()

    def weights_of(to_core, c, part):
        lanes = pl.ds(part * PART, PART)
        ratio = 1.0 + channel_ref[c].astype(F32) * (1.0 / 2048.0)
        gain_re = jnp.broadcast_to(gains_ref[c, 0:1, lanes] * (1.0 / 32.0), (16, PART))
        gain_im = jnp.broadcast_to(gains_ref[c, 1:2, lanes] * (1.0 / 32.0), (16, PART))
        real, imag = [], []
        for n in range(TURN_BEAMS // 16):
            at = pl.ds(pl.multiple_of(to_core * (BEAMS // 2) + n * 16, 16), 16)
            pair = weight_pair(geometry[at, lanes], ratio, gain_re, gain_im)
            real.append(pair[0].astype(BF16))
            imag.append(pair[1].astype(BF16))
        return jnp.concatenate(real + imag, axis=0)

    def intensity_of(product):
        beam_re = product[:TURN_BEAMS, :SAMPLES] - product[TURN_BEAMS:, SAMPLES:]
        beam_im = product[:TURN_BEAMS, SAMPLES:] + product[TURN_BEAMS:, :SAMPLES]
        power = beam_re * beam_re + beam_im * beam_im
        mean = jnp.sum(power, axis=1, keepdims=True) * (1.0 / SAMPLES)
        return 0.25 * (power - mean)

    def beams_of(to_core):
        parts = [(c, part) for c in range(CHANNELS) for part in range(ANTENNAS // PART)]
        ready, product = weights_of(to_core, *parts[0]), None
        for n, (c, part) in enumerate(parts):
            following = weights_of(to_core, *parts[n + 1]) if n + 1 < len(parts) else None
            term = jnp.dot(ready, volts[c, pl.ds(part * PART, PART), :], preferred_element_type=F32)
            product = term if part == 0 else product + term
            if part + 1 == ANTENNAS // PART:
                intensity[c] = intensity_of(product)
            ready = following
        for n in range(TURN_SENDS):
            for pair in range(CHANNELS // 2):
                rows = jnp.concatenate(
                    [intensity[2 * pair + c, n * OWN_BEAMS : (n + 1) * OWN_BEAMS, :] for c in range(2)], axis=0
                )
                outgoing[2 * n + to_core, pair * 16 : (pair + 1) * 16, :] = rows.astype(BF16)

    def shipment(distance, step, to_core):
        to = mate(distance, step, to_core)
        slot = (distance * GROUPS + step) * 2 + core
        return pltpu.make_async_remote_copy(
            src_ref=outgoing.at[to],
            dst_ref=incoming.at[slot],
            send_sem=send_sem,
            recv_sem=recv_sem.at[distance // 2],
            device_id=(to, freq_at),
            device_id_type=MESH,
        )

    def beams_and_send(to_core, carry):
        beams_of(to_core)

        @pl.when(to_core == 0)
        def _():
            pl.semaphore_wait(barrier, SENDERS - 1 + NEARS + FARS)

        for distance, step in ORDER[:-1]:
            shipment(distance, step, to_core).start()

        @pl.when(to_core != core)
        def _():
            shipment(0, 0, to_core).start()

        return carry

    lax.fori_loop(0, TURNS, beams_and_send, 0)
    keep = pltpu.make_async_copy(outgoing.at[beam_at], incoming.at[core], recv_sem.at[0])
    keep.start()

    lane = lax.broadcasted_iota(jnp.int32, (8, 128), 1)
    channel = (
        ((row + GROUPS - jnp.right_shift(lane, 5)) & (GROUPS - 1)) * (GROUP * CHANNELS)
        + ((spot + GROUPS - (jnp.right_shift(lane, 3) & (GROUPS - 1))) & (GROUPS - 1)) * (2 * CHANNELS)
        + (jnp.right_shift(lane, 2) & 1) * CHANNELS
        + (lane & (CHANNELS - 1))
    )
    delays = jnp.concatenate(
        [
            jnp.take_along_axis(delay_ref[8 * n : 8 * n + 8, :], channel, axis=1, mode="promise_in_bounds")
            for n in range(TRIALS // 8)
        ],
        axis=0,
    )
    selector[...] = jnp.concatenate(
        [jnp.where(delays == n, 1.0, 0.0) for n in range(OFFSETS)], axis=0
    ).astype(BF16)

    half_way = SENDERS // 2

    def all_blocks(first, count):
        return pltpu.make_async_remote_copy(
            src_ref=outgoing.at[pl.ds(first, count)],
            dst_ref=incoming.at[pl.ds(first, count)],
            send_sem=send_sem,
            recv_sem=recv_sem.at[first // half_way],
            device_id=(lax.rem(beam_at + 1, SENDERS), freq_at),
            device_id_type=MESH,
        )

    block_rows = CHANNELS * OWN_BEAMS

    def spread_columns(first, last):
        rows_f32[first * block_rows : last * block_rows, :] = (
            incoming[first:last].astype(F32).reshape((last - first) * block_rows, SAMPLES)
        )
        for b in range(OWN_BEAMS):
            columns[first * CHANNELS : last * CHANNELS, b * SAMPLES : (b + 1) * SAMPLES] = rows_f32[
                pl.ds(first * block_rows + b, (last - first) * CHANNELS, stride=OWN_BEAMS), :
            ].astype(BF16)

    all_blocks(half_way, half_way).wait_recv()
    spread_columns(half_way, SENDERS)
    all_blocks(0, half_way).wait_recv()
    spread_columns(0, half_way)

    time = lax.broadcasted_iota(jnp.int32, (TRIALS, SAMPLES), 1)
    for pair in range(OWN_BEAMS // 2):
        spread = jnp.dot(
            selector[...], columns[:, pair * 2 * SAMPLES : (pair + 1) * 2 * SAMPLES], preferred_element_type=F32
        )
        for side in range(2):
            total = spread[:TRIALS, side * SAMPLES : (side + 1) * SAMPLES]
            for n in range(1, OFFSETS):
                piece = spread[n * TRIALS : (n + 1) * TRIALS, side * SAMPLES : (side + 1) * SAMPLES]
                total = total + jnp.where(time >= n, pltpu.roll(piece, n, 1), 0.0)
            b = 2 * pair + side
            partial_f32[b * TRIALS : (b + 1) * TRIALS, :] = total
    for r in range(TRIALS):
        window[0, r] = partial_f32[pl.ds(r, OWN_BEAMS, stride=TRIALS), :]
    own_block[...] = window[0].reshape(TRIALS * OWN_BEAMS, SAMPLES).astype(BF16)

    nears = []
    for slot, offset in enumerate(near_offsets):
        near = pltpu.make_async_remote_copy(
            src_ref=own_block,
            dst_ref=window_in.at[slot],
            send_sem=near_send.at[slot],
            recv_sem=near_recv.at[slot],
            device_id=(beam_at, ring(-offset)),
            device_id_type=MESH,
        )
        near.start()
        nears.append(near)

    table_pad[...] = jnp.zeros_like(table_pad)
    table_pad[0:3, 0:ENTRIES] = merge_ref[...]
    code = table_pad[0:1, :] + 128 * table_pad[1:2, :] + 16384 * table_pad[2:3, :]
    pieces = [jnp.broadcast_to(code[:, 128 * n : 128 * (n + 1)], (8, 128)) for n in range(4)]
    turned = [pltpu.roll(piece, 32, 1) for piece in pieces]
    level_zero = pieces[0]
    level_one = pltpu.roll(pieces[0], 96, 1)
    level_two = jnp.where(lane < 32, turned[0], turned[1])
    last = [jnp.where(lane < 32, turned[1], turned[2]), jnp.where(lane < 32, turned[2], turned[3])]
    for part in range(2):
        subband = part * 8 + lax.broadcasted_iota(jnp.int32, (8, 128), 0)
        for half in range(2):
            found = last[half]
            late = jnp.zeros((8, 128), jnp.int32)
            for bit, level in ((3, level_two), (2, level_one), (1, level_zero), (0, None)):
                upper = lax.rem(jnp.right_shift(subband, bit), 2) == 1
                at = jnp.where(upper, jnp.right_shift(found, 7), found) & 127
                late = late + jnp.where(upper, jnp.right_shift(found, 14), 0)
                if level is not None:
                    found = jnp.take_along_axis(level, at, axis=1, mode="promise_in_bounds")
            table_vmem[pl.ds(part * 8, 8), pl.ds(half * 128, 128)] = at * 128 + late
    to_scalars = pltpu.make_async_copy(table_vmem, table, table_sem)
    to_scalars.start()

    def take_near(slot):
        nears[slot].wait_recv()
        window[slot + 1] = window_in[slot].astype(F32).reshape(TRIALS, OWN_BEAMS, SAMPLES)

    to_scalars.wait()
    take_near(0)
    take_near(1)
    subbands = [freq_at] + [ring(offset) for offset in near_offsets]
    moment = lax.broadcasted_iota(jnp.int32, (OWN_BEAMS, SAMPLES), 1)

    def window_sum(to, k, places):
        total = None
        for place in places:
            entry = table[subbands[place], to * TRIALS + k]
            late = entry & 127
            moved = pltpu.roll(window[place, jnp.right_shift(entry, 7) & (TRIALS - 1)], late, 1)
            moved = jnp.where(moment >= late, moved, 0.0)
            total = moved if total is None else total + moved
        return total

    far_to = [ring(-offset) for offset in far_offsets]

    def early_rows(k, carry):
        for f in range(FARS):
            early[f, k] = window_sum(far_to[f], k, (0, 1, 2))
        return carry

    lax.fori_loop(0, TRIALS, early_rows, 0, unroll=4)
    take_near(2)
    take_near(3)

    fars = []
    for f in range(FARS):

        def two_rows(n, carry, f=f):
            both = [early[f, k] + window_sum(far_to[f], k, (3, 4)) for k in (2 * n, 2 * n + 1)]
            sums_out[f, pl.ds(pl.multiple_of(n * 16, 16), 16), :] = jnp.concatenate(both, axis=0).astype(BF16)
            return carry

        lax.fori_loop(0, TRIALS // 2, two_rows, 0, unroll=True)
        far = pltpu.make_async_remote_copy(
            src_ref=sums_out.at[f],
            dst_ref=sums_in.at[f],
            send_sem=far_send.at[f],
            recv_sem=far_recv.at[f],
            device_id=(beam_at, far_to[f]),
            device_id_type=MESH,
        )
        far.start()
        fars.append(far)

    take_near(NEARS - 1)

    def own_rows(k, carry):
        out_ref[k] = window_sum(freq_at, k, range(PLACES))
        return carry

    lax.fori_loop(0, TRIALS, own_rows, 0, unroll=8)

    all_blocks(0, SENDERS - 1).wait_send()
    for near in nears:
        near.wait_send()
    for far in fars:
        far.wait()
    gathered = sums_in[0].astype(F32) + sums_in[1].astype(F32)
    out_ref[...] = (out_ref[...] + gathered.reshape(TRIALS, OWN_BEAMS, SAMPLES)) * (1.0 / math.sqrt(2048.0))


def on_device(voltages, gains, channel_map, positions, directions, local_delay, merge_table):
    received = SENDERS * CHANNELS * OWN_BEAMS
    block = TRIALS * OWN_BEAMS
    return pl.pallas_call(
        kernel,
        out_shape=pltpu.VMEM((TRIALS, OWN_BEAMS, SAMPLES), F32),
        in_specs=[pl.BlockSpec(memory_space=pl.ANY)] * 7,
        out_specs=pl.BlockSpec(memory_space=pltpu.VMEM),
        scratch_shapes=[
            pltpu.VMEM((CHANNELS, 2, ANTENNAS), F32),
            pltpu.SMEM((CHANNELS,), jnp.int32),
            pltpu.VMEM((2, ANTENNAS), F32),
            pltpu.VMEM((2, BEAMS), F32),
            pltpu.VMEM((TRIALS, SENDERS * CHANNELS), jnp.int32),
            pltpu.VMEM((3, ENTRIES), jnp.int32),
            pltpu.VMEM((CHANNELS, ANTENNAS, 2 * SAMPLES), BF16),
            pltpu.VMEM((BEAMS, ANTENNAS), F32),
            pltpu.VMEM((2, BEAMS, 128), F32),
            pltpu.VMEM((CHANNELS, TURN_BEAMS, SAMPLES), F32),
            pltpu.VMEM((SENDERS, CHANNELS * OWN_BEAMS, SAMPLES), BF16),
            pltpu.VMEM((SENDERS, CHANNELS * OWN_BEAMS, SAMPLES), BF16),
            pltpu.VMEM((received + OWN_BEAMS, SAMPLES), F32),
            pltpu.VMEM((SENDERS * CHANNELS, OWN_BEAMS * SAMPLES), BF16),
            pltpu.VMEM((OFFSETS * TRIALS, SENDERS * CHANNELS), BF16),
            pltpu.VMEM((block + TRIALS, SAMPLES), F32),
            pltpu.VMEM((PLACES, TRIALS, OWN_BEAMS, SAMPLES), F32),
            pltpu.VMEM((block, SAMPLES), BF16),
            pltpu.VMEM((NEARS, block, SAMPLES), BF16),
            pltpu.VMEM((FARS, block, SAMPLES), BF16),
            pltpu.VMEM((FARS, block, SAMPLES), BF16),
            pltpu.VMEM((FARS, TRIALS, OWN_BEAMS, SAMPLES), F32),
            pltpu.VMEM((8, 512), jnp.int32),
            pltpu.VMEM((SUBBANDS, 256), jnp.int32),
            pltpu.SMEM((SUBBANDS, 256), jnp.int32),
            pltpu.SemaphoreType.DMA((6,)),
            pltpu.SemaphoreType.DMA,
            pltpu.SemaphoreType.DMA,
            pltpu.SemaphoreType.DMA,
            pltpu.SemaphoreType.DMA((2,)),
            pltpu.SemaphoreType.DMA((NEARS,)),
            pltpu.SemaphoreType.DMA((NEARS,)),
            pltpu.SemaphoreType.DMA((FARS,)),
            pltpu.SemaphoreType.DMA((FARS,)),
        ],
        compiler_params=pltpu.CompilerParams(
            collective_id=0, has_side_effects=True, vmem_limit_bytes=48 * 2**20
        ),
        name="search_window",
    )(*[
        pltpu.with_memory_space_constraint(operand, pltpu.HBM)
        for operand in (voltages, gains, channel_map, positions, directions, local_delay, merge_table)
    ])


def solution(mesh):
    return jax.shard_map(
        on_device,
        mesh=mesh,
        in_specs=(
            P(("beam", "freq"), None, None),
            P(("beam", "freq"), None, None),
            P(("beam", "freq")),
            P(),
            P(),
            P("freq", None),
            P(),
        ),
        out_specs=P("freq", "beam", None),
        check_vma=False,
    )
```

```python
import functools
import math

import jax
import jax.numpy as jnp
from jax import lax
from jax.experimental import pallas as pl
from jax.experimental.pallas import tpu as pltpu
from jax.sharding import PartitionSpec as P

MESH = pl.DeviceIdType.MESH
F32 = jnp.float32
BF16 = jnp.bfloat16

CHANNELS = 4
ANTENNAS = 1024
BEAMS = 256
SAMPLES = 128
SENDERS = 32
GROUP = 8
GROUPS = SENDERS // GROUP
TURNS = 2
TURN_BEAMS = BEAMS // TURNS
TURN_SENDS = SENDERS // TURNS
OWN_BEAMS = BEAMS // SENDERS
TRIALS = 16
OFFSETS = 17
SUBBANDS = 16
REACH = 2
PLACES = 2 * REACH + 2
NEARS = PLACES - 1
FARS = 2
ENTRIES = 480
PART = 512
ORDER = (
    (2, 2), (3, 3), (2, 1), (3, 2), (2, 3), (3, 1), (2, 0), (3, 0),
    (1, 1), (0, 2), (1, 2), (0, 1), (1, 3), (0, 3), (1, 0), (0, 0),
)

SIN_TERMS = (2.641740790, -1.085953791, 0.130620464)
ROOT_TWO = math.sqrt(2.0)
ROUNDER = 12582912.0


def horner(terms, z):
    total = z * terms[-1] + terms[-2]
    for term in terms[-3::-1]:
        total = total * z + term
    return total


def weight_pair(geometry, ratio, gain_re, gain_im):
    turns = geometry * ratio
    rest = turns - ((turns + ROUNDER) - ROUNDER)
    z = rest * rest
    quarter_sin = rest * horner(SIN_TERMS, z)
    square = quarter_sin * quarter_sin
    left = 2.0 * ROOT_TWO - square
    half_sin = quarter_sin * (left * lax.rsqrt(left))
    cosine = 1.0 - half_sin * half_sin
    sine = half_sin * (ROOT_TWO - square)
    return gain_re * cosine + gain_im * sine, gain_im * cosine - gain_re * sine


def kernel(
    volts_hbm, gains_hbm, channel_hbm, positions_hbm, directions_hbm, delay_hbm, merge_hbm, out_ref,
    gains_ref, channel_ref, positions_ref, directions_ref, delay_ref, merge_ref, volts, geometry, across, intensity, outgoing, incoming, rows_f32, columns,
    selector, partial_f32, window, own_block, window_in, sums_out, sums_in, early, table_pad, table_vmem, table,
    small_sem, volts_sem, table_sem, send_sem, recv_sem, near_send, near_recv, far_send, far_recv,
):
    beam_at = lax.axis_index("beam")
    freq_at = lax.axis_index("freq")
    row = beam_at // GROUP
    spot = lax.rem(beam_at // 2, GROUPS)
    core = lax.rem(beam_at, 2)
    lean = 1 - 2 * core

    def ring(offset):
        return lax.rem(freq_at + offset + SUBBANDS, SUBBANDS)

    def mate(distance, step, to_core):
        return lax.rem(row + distance, GROUPS) * GROUP + lax.rem(spot + step, GROUPS) * 2 + to_core

    smalls = [
        pltpu.make_async_copy(src, dst, small_sem.at[n])
        for n, (src, dst) in enumerate((
            (directions_hbm, directions_ref), (positions_hbm, positions_ref), (gains_hbm, gains_ref),
            (channel_hbm, channel_ref), (delay_hbm, delay_ref), (merge_hbm, merge_ref),
        ))
    ]
    for small in smalls:
        small.start()
    load = pltpu.make_async_copy(volts_hbm, volts, volts_sem)
    load.start()

    barrier = pltpu.get_barrier_semaphore()

    for step in range(1, SENDERS):
        other = lax.rem(beam_at + step, SENDERS)
        pl.semaphore_signal(barrier, inc=1, device_id=(other, freq_at), device_id_type=MESH)
    near_offsets = (-1, 1, -2, 2, 3 * lean)
    far_offsets = (6 * lean, -5 * lean)
    for offset in near_offsets + far_offsets:
        pl.semaphore_signal(barrier, inc=1, device_id=(beam_at, ring(offset)), device_id_type=MESH)

    for small in smalls[:2]:
        small.wait()

    for k in range(2):
        across[k] = jnp.transpose(jnp.broadcast_to(directions_ref[k : k + 1, :], (128, BEAMS)))

    def geometry_rows(chip, carry):
        for to_core in range(2):
            at = pl.ds(pl.multiple_of(chip * 16 + to_core * 8, 8), 8)
            to = pl.ds(pl.multiple_of(to_core * (BEAMS // 2) + chip * 8, 8), 8)
            first, second = across[0, at, :], across[1, at, :]
            for n in range(ANTENNAS // 128):
                lanes = pl.ds(n * 128, 128)
                geometry[to, lanes] = (
                    first * positions_ref[0:1, lanes] + second * positions_ref[1:2, lanes]
                )
        return carry

    lax.fori_loop(0, SENDERS // 2, geometry_rows, 0)
    for small in smalls[2:]:
        small.wait()
    load.wait()

    def weights_of(to_core, c, part):
        lanes = pl.ds(part * PART, PART)
        ratio = 1.0 + channel_ref[c].astype(F32) * (1.0 / 2048.0)
        gain_re = jnp.broadcast_to(gains_ref[c, 0:1, lanes] * (1.0 / 32.0), (16, PART))
        gain_im = jnp.broadcast_to(gains_ref[c, 1:2, lanes] * (1.0 / 32.0), (16, PART))
        real, imag = [], []
        for n in range(TURN_BEAMS // 16):
            at = pl.ds(pl.multiple_of(to_core * (BEAMS // 2) + n * 16, 16), 16)
            pair = weight_pair(geometry[at, lanes], ratio, gain_re, gain_im)
            real.append(pair[0].astype(BF16))
            imag.append(pair[1].astype(BF16))
        return jnp.concatenate(real + imag, axis=0)

    def intensity_of(product):
        beam_re = product[:TURN_BEAMS, :SAMPLES] - product[TURN_BEAMS:, SAMPLES:]
        beam_im = product[:TURN_BEAMS, SAMPLES:] + product[TURN_BEAMS:, :SAMPLES]
        power = beam_re * beam_re + beam_im * beam_im
        mean = jnp.sum(power, axis=1, keepdims=True) * (1.0 / SAMPLES)
        return 0.25 * (power - mean)

    def beams_of(to_core):
        parts = [(c, part) for c in range(CHANNELS) for part in range(ANTENNAS // PART)]
        ready, product = weights_of(to_core, *parts[0]), None
        for n, (c, part) in enumerate(parts):
            following = weights_of(to_core, *parts[n + 1]) if n + 1 < len(parts) else None
            term = jnp.dot(ready, volts[c, pl.ds(part * PART, PART), :], preferred_element_type=F32)
            product = term if part == 0 else product + term
            if part + 1 == ANTENNAS // PART:
                intensity[c] = intensity_of(product)
            ready = following
        for n in range(TURN_SENDS):
            for pair in range(CHANNELS // 2):
                rows = jnp.concatenate(
                    [intensity[2 * pair + c, n * OWN_BEAMS : (n + 1) * OWN_BEAMS, :] for c in range(2)], axis=0
                )
                outgoing[2 * n + to_core, pair * 16 : (pair + 1) * 16, :] = rows.astype(BF16)

    def shipment(distance, step, to_core):
        to = mate(distance, step, to_core)
        slot = (distance * GROUPS + step) * 2 + core
        return pltpu.make_async_remote_copy(
            src_ref=outgoing.at[to],
            dst_ref=incoming.at[slot],
            send_sem=send_sem,
            recv_sem=recv_sem.at[distance // 2],
            device_id=(to, freq_at),
            device_id_type=MESH,
        )

    def beams_and_send(to_core, carry):
        beams_of(to_core)

        @pl.when(to_core == 0)
        def _():
            pl.semaphore_wait(barrier, SENDERS - 1 + NEARS + FARS)

        for distance, step in ORDER[:-1]:
            shipment(distance, step, to_core).start()

        @pl.when(to_core != core)
        def _():
            shipment(0, 0, to_core).start()

        return carry

    lax.fori_loop(0, TURNS, beams_and_send, 0)
    keep = pltpu.make_async_copy(outgoing.at[beam_at], incoming.at[core], recv_sem.at[0])
    keep.start()

    lane = lax.broadcasted_iota(jnp.int32, (8, 128), 1)
    channel = (
        ((row + GROUPS - jnp.right_shift(lane, 5)) & (GROUPS - 1)) * (GROUP * CHANNELS)
        + ((spot + GROUPS - (jnp.right_shift(lane, 3) & (GROUPS - 1))) & (GROUPS - 1)) * (2 * CHANNELS)
        + (jnp.right_shift(lane, 2) & 1) * CHANNELS
        + (lane & (CHANNELS - 1))
    )
    delays = jnp.concatenate(
        [
            jnp.take_along_axis(delay_ref[8 * n : 8 * n + 8, :], channel, axis=1, mode="promise_in_bounds")
            for n in range(TRIALS // 8)
        ],
        axis=0,
    )
    selector[...] = jnp.concatenate(
        [jnp.where(delays == n, 1.0, 0.0) for n in range(OFFSETS)], axis=0
    ).astype(BF16)

    half_way = SENDERS // 2

    def all_blocks(first, count):
        return pltpu.make_async_remote_copy(
            src_ref=outgoing.at[pl.ds(first, count)],
            dst_ref=incoming.at[pl.ds(first, count)],
            send_sem=send_sem,
            recv_sem=recv_sem.at[first // half_way],
            device_id=(lax.rem(beam_at + 1, SENDERS), freq_at),
            device_id_type=MESH,
        )

    block_rows = CHANNELS * OWN_BEAMS

    def spread_columns(first, last):
        rows_f32[first * block_rows : last * block_rows, :] = (
            incoming[first:last].astype(F32).reshape((last - first) * block_rows, SAMPLES)
        )
        for b in range(OWN_BEAMS):
            columns[first * CHANNELS : last * CHANNELS, b * SAMPLES : (b + 1) * SAMPLES] = rows_f32[
                pl.ds(first * block_rows + b, (last - first) * CHANNELS, stride=OWN_BEAMS), :
            ].astype(BF16)

    all_blocks(half_way, half_way).wait_recv()
    spread_columns(half_way, SENDERS)
    all_blocks(0, half_way).wait_recv()
    spread_columns(0, half_way)

    time = lax.broadcasted_iota(jnp.int32, (TRIALS, SAMPLES), 1)
    for pair in range(OWN_BEAMS // 2):
        spread = jnp.dot(
            selector[...], columns[:, pair * 2 * SAMPLES : (pair + 1) * 2 * SAMPLES], preferred_element_type=F32
        )
        for side in range(2):
            total = spread[:TRIALS, side * SAMPLES : (side + 1) * SAMPLES]
            for n in range(1, OFFSETS):
                piece = spread[n * TRIALS : (n + 1) * TRIALS, side * SAMPLES : (side + 1) * SAMPLES]
                total = total + jnp.where(time >= n, pltpu.roll(piece, n, 1), 0.0)
            b = 2 * pair + side
            partial_f32[b * TRIALS : (b + 1) * TRIALS, :] = total
    for r in range(TRIALS):
        window[0, r] = partial_f32[pl.ds(r, OWN_BEAMS, stride=TRIALS), :]
    own_block[...] = window[0].reshape(TRIALS * OWN_BEAMS, SAMPLES).astype(BF16)

    nears = []
    for slot, offset in enumerate(near_offsets):
        near = pltpu.make_async_remote_copy(
            src_ref=own_block,
            dst_ref=window_in.at[slot],
            send_sem=near_send.at[slot],
            recv_sem=near_recv.at[slot],
            device_id=(beam_at, ring(-offset)),
            device_id_type=MESH,
        )
        near.start()
        nears.append(near)

    table_pad[...] = jnp.zeros_like(table_pad)
    table_pad[0:3, 0:ENTRIES] = merge_ref[...]
    code = table_pad[0:1, :] + 128 * table_pad[1:2, :] + 16384 * table_pad[2:3, :]
    pieces = [jnp.broadcast_to(code[:, 128 * n : 128 * (n + 1)], (8, 128)) for n in range(4)]
    turned = [pltpu.roll(piece, 32, 1) for piece in pieces]
    level_zero = pieces[0]
    level_one = pltpu.roll(pieces[0], 96, 1)
    level_two = jnp.where(lane < 32, turned[0], turned[1])
    last = [jnp.where(lane < 32, turned[1], turned[2]), jnp.where(lane < 32, turned[2], turned[3])]
    for part in range(2):
        subband = part * 8 + lax.broadcasted_iota(jnp.int32, (8, 128), 0)
        for half in range(2):
            found = last[half]
            late = jnp.zeros((8, 128), jnp.int32)
            for bit, level in ((3, level_two), (2, level_one), (1, level_zero), (0, None)):
                upper = lax.rem(jnp.right_shift(subband, bit), 2) == 1
                at = jnp.where(upper, jnp.right_shift(found, 7), found) & 127
                late = late + jnp.where(upper, jnp.right_shift(found, 14), 0)
                if level is not None:
                    found = jnp.take_along_axis(level, at, axis=1, mode="promise_in_bounds")
            table_vmem[pl.ds(part * 8, 8), pl.ds(half * 128, 128)] = at * 128 + late
    to_scalars = pltpu.make_async_copy(table_vmem, table, table_sem)
    to_scalars.start()

    def take_near(slot):
        nears[slot].wait_recv()
        window[slot + 1] = window_in[slot].astype(F32).reshape(TRIALS, OWN_BEAMS, SAMPLES)

    to_scalars.wait()
    take_near(0)
    take_near(1)
    subbands = [freq_at] + [ring(offset) for offset in near_offsets]
    moment = lax.broadcasted_iota(jnp.int32, (OWN_BEAMS, SAMPLES), 1)

    def window_sum(to, k, places):
        total = None
        for place in places:
            entry = table[subbands[place], to * TRIALS + k]
            late = entry & 127
            moved = pltpu.roll(window[place, jnp.right_shift(entry, 7) & (TRIALS - 1)], late, 1)
            moved = jnp.where(moment >= late, moved, 0.0)
            total = moved if total is None else total + moved
        return total

    far_to = [ring(-offset) for offset in far_offsets]

    def early_rows(k, carry):
        for f in range(FARS):
            early[f, k] = window_sum(far_to[f], k, (0, 1, 2))
        return carry

    lax.fori_loop(0, TRIALS, early_rows, 0, unroll=8)
    take_near(2)
    take_near(3)

    fars = []
    for f in range(FARS):

        def two_rows(n, carry, f=f):
            both = [early[f, k] + window_sum(far_to[f], k, (3, 4)) for k in (2 * n, 2 * n + 1)]
            sums_out[f, pl.ds(pl.multiple_of(n * 16, 16), 16), :] = jnp.concatenate(both, axis=0).astype(BF16)
            return carry

        lax.fori_loop(0, TRIALS // 2, two_rows, 0, unroll=True)
        far = pltpu.make_async_remote_copy(
            src_ref=sums_out.at[f],
            dst_ref=sums_in.at[f],
            send_sem=far_send.at[f],
            recv_sem=far_recv.at[f],
            device_id=(beam_at, far_to[f]),
            device_id_type=MESH,
        )
        far.start()
        fars.append(far)

    take_near(NEARS - 1)

    def own_rows(k, carry):
        out_ref[k] = window_sum(freq_at, k, range(PLACES))
        return carry

    lax.fori_loop(0, TRIALS, own_rows, 0, unroll=8)

    all_blocks(0, SENDERS - 1).wait_send()
    for near in nears:
        near.wait_send()
    for far in fars:
        far.wait()
    gathered = sums_in[0].astype(F32) + sums_in[1].astype(F32)
    out_ref[...] = (out_ref[...] + gathered.reshape(TRIALS, OWN_BEAMS, SAMPLES)) * (1.0 / math.sqrt(2048.0))


def on_device(voltages, gains, channel_map, positions, directions, local_delay, merge_table):
    received = SENDERS * CHANNELS * OWN_BEAMS
    block = TRIALS * OWN_BEAMS
    return pl.pallas_call(
        kernel,
        out_shape=pltpu.VMEM((TRIALS, OWN_BEAMS, SAMPLES), F32),
        in_specs=[pl.BlockSpec(memory_space=pl.ANY)] * 7,
        out_specs=pl.BlockSpec(memory_space=pltpu.VMEM),
        scratch_shapes=[
            pltpu.VMEM((CHANNELS, 2, ANTENNAS), F32),
            pltpu.SMEM((CHANNELS,), jnp.int32),
            pltpu.VMEM((2, ANTENNAS), F32),
            pltpu.VMEM((2, BEAMS), F32),
            pltpu.VMEM((TRIALS, SENDERS * CHANNELS), jnp.int32),
            pltpu.VMEM((3, ENTRIES), jnp.int32),
            pltpu.VMEM((CHANNELS, ANTENNAS, 2 * SAMPLES), BF16),
            pltpu.VMEM((BEAMS, ANTENNAS), F32),
            pltpu.VMEM((2, BEAMS, 128), F32),
            pltpu.VMEM((CHANNELS, TURN_BEAMS, SAMPLES), F32),
            pltpu.VMEM((SENDERS, CHANNELS * OWN_BEAMS, SAMPLES), BF16),
            pltpu.VMEM((SENDERS, CHANNELS * OWN_BEAMS, SAMPLES), BF16),
            pltpu.VMEM((received + OWN_BEAMS, SAMPLES), F32),
            pltpu.VMEM((SENDERS * CHANNELS, OWN_BEAMS * SAMPLES), BF16),
            pltpu.VMEM((OFFSETS * TRIALS, SENDERS * CHANNELS), BF16),
            pltpu.VMEM((block + TRIALS, SAMPLES), F32),
            pltpu.VMEM((PLACES, TRIALS, OWN_BEAMS, SAMPLES), F32),
            pltpu.VMEM((block, SAMPLES), BF16),
            pltpu.VMEM((NEARS, block, SAMPLES), BF16),
            pltpu.VMEM((FARS, block, SAMPLES), BF16),
            pltpu.VMEM((FARS, block, SAMPLES), BF16),
            pltpu.VMEM((FARS, TRIALS, OWN_BEAMS, SAMPLES), F32),
            pltpu.VMEM((8, 512), jnp.int32),
            pltpu.VMEM((SUBBANDS, 256), jnp.int32),
            pltpu.SMEM((SUBBANDS, 256), jnp.int32),
            pltpu.SemaphoreType.DMA((6,)),
            pltpu.SemaphoreType.DMA,
            pltpu.SemaphoreType.DMA,
            pltpu.SemaphoreType.DMA,
            pltpu.SemaphoreType.DMA((2,)),
            pltpu.SemaphoreType.DMA((NEARS,)),
            pltpu.SemaphoreType.DMA((NEARS,)),
            pltpu.SemaphoreType.DMA((FARS,)),
            pltpu.SemaphoreType.DMA((FARS,)),
        ],
        compiler_params=pltpu.CompilerParams(
            collective_id=0, has_side_effects=True, vmem_limit_bytes=48 * 2**20
        ),
        name="search_window",
    )(*[
        pltpu.with_memory_space_constraint(operand, pltpu.HBM)
        for operand in (voltages, gains, channel_map, positions, directions, local_delay, merge_table)
    ])


def solution(mesh):
    return jax.shard_map(
        on_device,
        mesh=mesh,
        in_specs=(
            P(("beam", "freq"), None, None),
            P(("beam", "freq"), None, None),
            P(("beam", "freq")),
            P(),
            P(),
            P("freq", None),
            P(),
        ),
        out_specs=P("freq", "beam", None),
        check_vma=False,
    )
```

```python
import functools
import math

import jax
import jax.numpy as jnp
from jax import lax
from jax.experimental import pallas as pl
from jax.experimental.pallas import tpu as pltpu
from jax.sharding import PartitionSpec as P

MESH = pl.DeviceIdType.MESH
F32 = jnp.float32
BF16 = jnp.bfloat16

CHANNELS = 4
ANTENNAS = 1024
BEAMS = 256
SAMPLES = 128
SENDERS = 32
GROUP = 8
GROUPS = SENDERS // GROUP
TURNS = 2
TURN_BEAMS = BEAMS // TURNS
TURN_SENDS = SENDERS // TURNS
OWN_BEAMS = BEAMS // SENDERS
TRIALS = 16
OFFSETS = 17
SUBBANDS = 16
REACH = 2
PLACES = 2 * REACH + 2
NEARS = PLACES - 1
FARS = 2
ENTRIES = 480
PART = 512
ORDER = (
    (2, 2), (3, 3), (2, 1), (3, 2), (2, 3), (3, 1), (2, 0), (3, 0),
    (1, 1), (0, 2), (1, 2), (0, 1), (1, 3), (0, 3), (1, 0), (0, 0),
)

SIN_TERMS = (2.641740790, -1.085953791, 0.130620464)
ROOT_TWO = math.sqrt(2.0)
ROUNDER = 12582912.0


def horner(terms, z):
    total = z * terms[-1] + terms[-2]
    for term in terms[-3::-1]:
        total = total * z + term
    return total


def weight_pair(geometry, ratio, gain_re, gain_im):
    turns = geometry * ratio
    rest = turns - ((turns + ROUNDER) - ROUNDER)
    z = rest * rest
    quarter_sin = rest * horner(SIN_TERMS, z)
    square = quarter_sin * quarter_sin
    left = 2.0 * ROOT_TWO - square
    half_sin = quarter_sin * (left * lax.rsqrt(left))
    cosine = 1.0 - half_sin * half_sin
    sine = half_sin * (ROOT_TWO - square)
    return gain_re * cosine + gain_im * sine, gain_im * cosine - gain_re * sine


def kernel(
    volts_hbm, gains_hbm, channel_hbm, positions_hbm, directions_hbm, delay_hbm, merge_hbm, out_ref,
    gains_ref, channel_ref, positions_ref, directions_ref, delay_ref, merge_ref, volts, geometry, across, intensity, outgoing, incoming, rows_f32, columns,
    selector, partial_f32, window, own_block, window_in, sums_out, sums_in, early, table_pad, table_vmem, table,
    small_sem, volts_sem, table_sem, send_sem, recv_sem, near_send, near_recv, far_send, far_recv,
):
    beam_at = lax.axis_index("beam")
    freq_at = lax.axis_index("freq")
    row = beam_at // GROUP
    spot = lax.rem(beam_at // 2, GROUPS)
    core = lax.rem(beam_at, 2)
    lean = 1 - 2 * core

    def ring(offset):
        return lax.rem(freq_at + offset + SUBBANDS, SUBBANDS)

    def mate(distance, step, to_core):
        return lax.rem(row + distance, GROUPS) * GROUP + lax.rem(spot + step, GROUPS) * 2 + to_core

    smalls = [
        pltpu.make_async_copy(src, dst, small_sem.at[n])
        for n, (src, dst) in enumerate((
            (directions_hbm, directions_ref), (positions_hbm, positions_ref), (gains_hbm, gains_ref),
            (channel_hbm, channel_ref), (delay_hbm, delay_ref), (merge_hbm, merge_ref),
        ))
    ]
    for small in smalls:
        small.start()
    load = pltpu.make_async_copy(volts_hbm, volts, volts_sem)
    load.start()

    barrier = pltpu.get_barrier_semaphore()

    for step in range(1, SENDERS):
        other = lax.rem(beam_at + step, SENDERS)
        pl.semaphore_signal(barrier, inc=1, device_id=(other, freq_at), device_id_type=MESH)
    near_offsets = (-1, 1, -2, 2, 3 * lean)
    far_offsets = (6 * lean, -5 * lean)
    for offset in near_offsets + far_offsets:
        pl.semaphore_signal(barrier, inc=1, device_id=(beam_at, ring(offset)), device_id_type=MESH)

    for small in smalls[:2]:
        small.wait()

    for k in range(2):
        across[k] = jnp.transpose(jnp.broadcast_to(directions_ref[k : k + 1, :], (128, BEAMS)))

    def geometry_rows(chip, carry):
        for to_core in range(2):
            at = pl.ds(pl.multiple_of(chip * 16 + to_core * 8, 8), 8)
            to = pl.ds(pl.multiple_of(to_core * (BEAMS // 2) + chip * 8, 8), 8)
            first, second = across[0, at, :], across[1, at, :]
            for n in range(ANTENNAS // 128):
                lanes = pl.ds(n * 128, 128)
                geometry[to, lanes] = (
                    first * positions_ref[0:1, lanes] + second * positions_ref[1:2, lanes]
                )
        return carry

    lax.fori_loop(0, SENDERS // 2, geometry_rows, 0)
    for small in smalls[2:]:
        small.wait()
    load.wait()

    def weights_of(to_core, c, part):
        lanes = pl.ds(part * PART, PART)
        ratio = 1.0 + channel_ref[c].astype(F32) * (1.0 / 2048.0)
        gain_re = jnp.broadcast_to(gains_ref[c, 0:1, lanes] * (1.0 / 32.0), (16, PART))
        gain_im = jnp.broadcast_to(gains_ref[c, 1:2, lanes] * (1.0 / 32.0), (16, PART))
        real, imag = [], []
        for n in range(TURN_BEAMS // 16):
            at = pl.ds(pl.multiple_of(to_core * (BEAMS // 2) + n * 16, 16), 16)
            pair = weight_pair(geometry[at, lanes], ratio, gain_re, gain_im)
            real.append(pair[0].astype(BF16))
            imag.append(pair[1].astype(BF16))
        return jnp.concatenate(real + imag, axis=0)

    def intensity_of(product):
        beam_re = product[:TURN_BEAMS, :SAMPLES] - product[TURN_BEAMS:, SAMPLES:]
        beam_im = product[:TURN_BEAMS, SAMPLES:] + product[TURN_BEAMS:, :SAMPLES]
        power = beam_re * beam_re + beam_im * beam_im
        mean = jnp.sum(power, axis=1, keepdims=True) * (1.0 / SAMPLES)
        return 0.25 * (power - mean)

    def beams_of(to_core):
        parts = [(c, part) for c in range(CHANNELS) for part in range(ANTENNAS // PART)]
        ready, product = weights_of(to_core, *parts[0]), None
        for n, (c, part) in enumerate(parts):
            following = weights_of(to_core, *parts[n + 1]) if n + 1 < len(parts) else None
            term = jnp.dot(ready, volts[c, pl.ds(part * PART, PART), :], preferred_element_type=F32)
            product = term if part == 0 else product + term
            if part + 1 == ANTENNAS // PART:
                intensity[c] = intensity_of(product)
            ready = following
        for n in range(TURN_SENDS):
            for pair in range(CHANNELS // 2):
                rows = jnp.concatenate(
                    [intensity[2 * pair + c, n * OWN_BEAMS : (n + 1) * OWN_BEAMS, :] for c in range(2)], axis=0
                )
                outgoing[2 * n + to_core, pair * 16 : (pair + 1) * 16, :] = rows.astype(BF16)

    def shipment(distance, step, to_core):
        to = mate(distance, step, to_core)
        slot = (distance * GROUPS + step) * 2 + core
        return pltpu.make_async_remote_copy(
            src_ref=outgoing.at[to],
            dst_ref=incoming.at[slot],
            send_sem=send_sem,
            recv_sem=recv_sem.at[distance // 2],
            device_id=(to, freq_at),
            device_id_type=MESH,
        )

    def beams_and_send(to_core, carry):
        beams_of(to_core)

        @pl.when(to_core == 0)
        def _():
            pl.semaphore_wait(barrier, SENDERS - 1 + NEARS + FARS)

        for distance, step in ORDER[:-1]:
            shipment(distance, step, to_core).start()

        @pl.when(to_core != core)
        def _():
            shipment(0, 0, to_core).start()

        return carry

    lax.fori_loop(0, TURNS, beams_and_send, 0)
    keep = pltpu.make_async_copy(outgoing.at[beam_at], incoming.at[core], recv_sem.at[0])
    keep.start()

    lane = lax.broadcasted_iota(jnp.int32, (8, 128), 1)
    channel = (
        ((row + GROUPS - jnp.right_shift(lane, 5)) & (GROUPS - 1)) * (GROUP * CHANNELS)
        + ((spot + GROUPS - (jnp.right_shift(lane, 3) & (GROUPS - 1))) & (GROUPS - 1)) * (2 * CHANNELS)
        + (jnp.right_shift(lane, 2) & 1) * CHANNELS
        + (lane & (CHANNELS - 1))
    )
    delays = jnp.concatenate(
        [
            jnp.take_along_axis(delay_ref[8 * n : 8 * n + 8, :], channel, axis=1, mode="promise_in_bounds")
            for n in range(TRIALS // 8)
        ],
        axis=0,
    )
    selector[...] = jnp.concatenate(
        [jnp.where(delays == n, 1.0, 0.0) for n in range(OFFSETS)], axis=0
    ).astype(BF16)

    half_way = SENDERS // 2

    def all_blocks(first, count):
        return pltpu.make_async_remote_copy(
            src_ref=outgoing.at[pl.ds(first, count)],
            dst_ref=incoming.at[pl.ds(first, count)],
            send_sem=send_sem,
            recv_sem=recv_sem.at[first // half_way],
            device_id=(lax.rem(beam_at + 1, SENDERS), freq_at),
            device_id_type=MESH,
        )

    block_rows = CHANNELS * OWN_BEAMS

    def spread_columns(first, last):
        rows_f32[first * block_rows : last * block_rows, :] = (
            incoming[first:last].astype(F32).reshape((last - first) * block_rows, SAMPLES)
        )
        for b in range(OWN_BEAMS):
            columns[first * CHANNELS : last * CHANNELS, b * SAMPLES : (b + 1) * SAMPLES] = rows_f32[
                pl.ds(first * block_rows + b, (last - first) * CHANNELS, stride=OWN_BEAMS), :
            ].astype(BF16)

    all_blocks(half_way, half_way).wait_recv()
    spread_columns(half_way, SENDERS)
    all_blocks(0, half_way).wait_recv()
    spread_columns(0, half_way)

    time = lax.broadcasted_iota(jnp.int32, (TRIALS, SAMPLES), 1)
    for pair in range(OWN_BEAMS // 2):
        spread = jnp.dot(
            selector[...], columns[:, pair * 2 * SAMPLES : (pair + 1) * 2 * SAMPLES], preferred_element_type=F32
        )
        for side in range(2):
            total = spread[:TRIALS, side * SAMPLES : (side + 1) * SAMPLES]
            for n in range(1, OFFSETS):
                piece = spread[n * TRIALS : (n + 1) * TRIALS, side * SAMPLES : (side + 1) * SAMPLES]
                total = total + jnp.where(time >= n, pltpu.roll(piece, n, 1), 0.0)
            b = 2 * pair + side
            partial_f32[b * TRIALS : (b + 1) * TRIALS, :] = total
    for r in range(TRIALS):
        window[0, r] = partial_f32[pl.ds(r, OWN_BEAMS, stride=TRIALS), :]
    own_block[...] = window[0].reshape(TRIALS * OWN_BEAMS, SAMPLES).astype(BF16)

    nears = []
    for slot, offset in enumerate(near_offsets):
        near = pltpu.make_async_remote_copy(
            src_ref=own_block,
            dst_ref=window_in.at[slot],
            send_sem=near_send.at[slot],
            recv_sem=near_recv.at[slot],
            device_id=(beam_at, ring(-offset)),
            device_id_type=MESH,
        )
        near.start()
        nears.append(near)

    table_pad[...] = jnp.zeros_like(table_pad)
    table_pad[0:3, 0:ENTRIES] = merge_ref[...]
    code = table_pad[0:1, :] + 128 * table_pad[1:2, :] + 16384 * table_pad[2:3, :]
    pieces = [jnp.broadcast_to(code[:, 128 * n : 128 * (n + 1)], (8, 128)) for n in range(4)]
    turned = [pltpu.roll(piece, 32, 1) for piece in pieces]
    level_zero = pieces[0]
    level_one = pltpu.roll(pieces[0], 96, 1)
    level_two = jnp.where(lane < 32, turned[0], turned[1])
    last = [jnp.where(lane < 32, turned[1], turned[2]), jnp.where(lane < 32, turned[2], turned[3])]
    for part in range(2):
        subband = part * 8 + lax.broadcasted_iota(jnp.int32, (8, 128), 0)
        for half in range(2):
            found = last[half]
            late = jnp.zeros((8, 128), jnp.int32)
            for bit, level in ((3, level_two), (2, level_one), (1, level_zero), (0, None)):
                upper = lax.rem(jnp.right_shift(subband, bit), 2) == 1
                at = jnp.where(upper, jnp.right_shift(found, 7), found) & 127
                late = late + jnp.where(upper, jnp.right_shift(found, 14), 0)
                if level is not None:
                    found = jnp.take_along_axis(level, at, axis=1, mode="promise_in_bounds")
            table_vmem[pl.ds(part * 8, 8), pl.ds(half * 128, 128)] = at * 128 + late
    to_scalars = pltpu.make_async_copy(table_vmem, table, table_sem)
    to_scalars.start()

    def take_near(slot):
        nears[slot].wait_recv()
        window[slot + 1] = window_in[slot].astype(F32).reshape(TRIALS, OWN_BEAMS, SAMPLES)

    to_scalars.wait()
    take_near(0)
    take_near(1)
    subbands = [freq_at] + [ring(offset) for offset in near_offsets]
    moment = lax.broadcasted_iota(jnp.int32, (OWN_BEAMS, SAMPLES), 1)

    def window_sum(to, k, places):
        total = None
        for place in places:
            entry = table[subbands[place], to * TRIALS + k]
            late = entry & 127
            moved = pltpu.roll(window[place, jnp.right_shift(entry, 7) & (TRIALS - 1)], late, 1)
            moved = jnp.where(moment >= late, moved, 0.0)
            total = moved if total is None else total + moved
        return total

    far_to = [ring(-offset) for offset in far_offsets]

    def early_rows(k, carry):
        for f in range(FARS):
            early[f, k] = window_sum(far_to[f], k, (0, 1, 2))
        return carry

    lax.fori_loop(0, TRIALS, early_rows, 0, unroll=16)
    take_near(2)
    take_near(3)

    fars = []
    for f in range(FARS):

        def two_rows(n, carry, f=f):
            both = [early[f, k] + window_sum(far_to[f], k, (3, 4)) for k in (2 * n, 2 * n + 1)]
            sums_out[f, pl.ds(pl.multiple_of(n * 16, 16), 16), :] = jnp.concatenate(both, axis=0).astype(BF16)
            return carry

        lax.fori_loop(0, TRIALS // 2, two_rows, 0, unroll=True)
        far = pltpu.make_async_remote_copy(
            src_ref=sums_out.at[f],
            dst_ref=sums_in.at[f],
            send_sem=far_send.at[f],
            recv_sem=far_recv.at[f],
            device_id=(beam_at, far_to[f]),
            device_id_type=MESH,
        )
        far.start()
        fars.append(far)

    take_near(NEARS - 1)

    def own_rows(k, carry):
        out_ref[k] = window_sum(freq_at, k, range(PLACES))
        return carry

    lax.fori_loop(0, TRIALS, own_rows, 0, unroll=8)

    all_blocks(0, SENDERS - 1).wait_send()
    for near in nears:
        near.wait_send()
    for far in fars:
        far.wait()
    gathered = sums_in[0].astype(F32) + sums_in[1].astype(F32)
    out_ref[...] = (out_ref[...] + gathered.reshape(TRIALS, OWN_BEAMS, SAMPLES)) * (1.0 / math.sqrt(2048.0))


def on_device(voltages, gains, channel_map, positions, directions, local_delay, merge_table):
    received = SENDERS * CHANNELS * OWN_BEAMS
    block = TRIALS * OWN_BEAMS
    return pl.pallas_call(
        kernel,
        out_shape=pltpu.VMEM((TRIALS, OWN_BEAMS, SAMPLES), F32),
        in_specs=[pl.BlockSpec(memory_space=pl.ANY)] * 7,
        out_specs=pl.BlockSpec(memory_space=pltpu.VMEM),
        scratch_shapes=[
            pltpu.VMEM((CHANNELS, 2, ANTENNAS), F32),
            pltpu.SMEM((CHANNELS,), jnp.int32),
            pltpu.VMEM((2, ANTENNAS), F32),
            pltpu.VMEM((2, BEAMS), F32),
            pltpu.VMEM((TRIALS, SENDERS * CHANNELS), jnp.int32),
            pltpu.VMEM((3, ENTRIES), jnp.int32),
            pltpu.VMEM((CHANNELS, ANTENNAS, 2 * SAMPLES), BF16),
            pltpu.VMEM((BEAMS, ANTENNAS), F32),
            pltpu.VMEM((2, BEAMS, 128), F32),
            pltpu.VMEM((CHANNELS, TURN_BEAMS, SAMPLES), F32),
            pltpu.VMEM((SENDERS, CHANNELS * OWN_BEAMS, SAMPLES), BF16),
            pltpu.VMEM((SENDERS, CHANNELS * OWN_BEAMS, SAMPLES), BF16),
            pltpu.VMEM((received + OWN_BEAMS, SAMPLES), F32),
            pltpu.VMEM((SENDERS * CHANNELS, OWN_BEAMS * SAMPLES), BF16),
            pltpu.VMEM((OFFSETS * TRIALS, SENDERS * CHANNELS), BF16),
            pltpu.VMEM((block + TRIALS, SAMPLES), F32),
            pltpu.VMEM((PLACES, TRIALS, OWN_BEAMS, SAMPLES), F32),
            pltpu.VMEM((block, SAMPLES), BF16),
            pltpu.VMEM((NEARS, block, SAMPLES), BF16),
            pltpu.VMEM((FARS, block, SAMPLES), BF16),
            pltpu.VMEM((FARS, block, SAMPLES), BF16),
            pltpu.VMEM((FARS, TRIALS, OWN_BEAMS, SAMPLES), F32),
            pltpu.VMEM((8, 512), jnp.int32),
            pltpu.VMEM((SUBBANDS, 256), jnp.int32),
            pltpu.SMEM((SUBBANDS, 256), jnp.int32),
            pltpu.SemaphoreType.DMA((6,)),
            pltpu.SemaphoreType.DMA,
            pltpu.SemaphoreType.DMA,
            pltpu.SemaphoreType.DMA,
            pltpu.SemaphoreType.DMA((2,)),
            pltpu.SemaphoreType.DMA((NEARS,)),
            pltpu.SemaphoreType.DMA((NEARS,)),
            pltpu.SemaphoreType.DMA((FARS,)),
            pltpu.SemaphoreType.DMA((FARS,)),
        ],
        compiler_params=pltpu.CompilerParams(
            collective_id=0, has_side_effects=True, vmem_limit_bytes=48 * 2**20
        ),
        name="search_window",
    )(*[
        pltpu.with_memory_space_constraint(operand, pltpu.HBM)
        for operand in (voltages, gains, channel_map, positions, directions, local_delay, merge_table)
    ])


def solution(mesh):
    return jax.shard_map(
        on_device,
        mesh=mesh,
        in_specs=(
            P(("beam", "freq"), None, None),
            P(("beam", "freq"), None, None),
            P(("beam", "freq")),
            P(),
            P(),
            P("freq", None),
            P(),
        ),
        out_specs=P("freq", "beam", None),
        check_vma=False,
    )
```
